256 devices in a mesh: ctx: 32 (over y, x, core), head: 8 (over z).
Axes of the slice: x: 4, y: 4, z: 8, core: 2. Of those that a mesh axis runs over, the one named last changes fastest.
Arguments:
- latents: bfloat16 [131072, 576], P('ctx'), may hold values from -8 to 8
- idx_keys: bfloat16 [131072, 128], P('ctx'), may hold values from -8 to 8
- mla_query: bfloat16 [4096, 128, 576], P('ctx', 'head'), may hold values from -32 to 32
- idx_query: bfloat16 [4096, 64, 128], P('ctx', 'head'), may hold values from -100 to 100
- idx_weight: bfloat16 [4096, 64], P('ctx', 'head'), may hold values from -1.5 to 1.5
- sel_blocks: int32 [64, 32], P('ctx'), may hold values from 0 to 2047, as said below
Outputs:
- kl: float32 [4096], P(('ctx', 'head'))
- grad_query: float32 [4096, 64, 128], P('ctx', 'head')
- grad_weight: float32 [4096, 64], P('ctx', 'head')
- grad_keys: float32 [2048, 64, 128], P('ctx', 'head')
The draws below stay inside these ranges and needn't reach their ends.
Inputs may be any that keep to these rules, and one draw needn't show every extreme that they name: `sel_blocks`: row r lists 32 different key blocks, none after block 1984 + r. At most 2 of a row's blocks lie in the range of 4096 keys of one index of ctx, and in every draw one such range holds exactly 2 blocks of every row.
All inputs are finite; a program needn't handle non-finite values.
Results may differ from the reference program's by a relative error of at most 0.018.
Values may be sent and summed in bfloat16 or wider, within the bound.
A program may use at most 128 MiB of HBM per device.

```python
import jax
import jax.numpy as jnp
from jax import lax

HEADS = 128
LAT = 576
IHEADS = 64
DI = 128
BLK = 64
SEL = 32
KEY_DEV = 4096
CAP = 2
CONTEXT = 131072
QUERIES = 4096
N_CTX = 32


def draw_latents(key, part):
    key = jax.random.fold_in(key, 1)
    values = jax.random.normal(key, (CONTEXT, LAT), jnp.float32)
    return jnp.clip(values, -8.0, 8.0).astype(jnp.bfloat16)


def draw_idx_keys(key, part):
    key = jax.random.fold_in(key, 2)
    values = jax.random.normal(key, (CONTEXT, DI), jnp.float32)
    return jnp.clip(values, -8.0, 8.0).astype(jnp.bfloat16)


def draw_mla_query(key, part):
    key = jax.random.fold_in(key, 3)
    noise = jax.random.normal(key, (QUERIES, HEADS, LAT), jnp.float32)
    values = noise
    return jnp.clip(values, -32.0, 32.0).astype(jnp.bfloat16)


def draw_idx_query(key, part):
    key = jax.random.fold_in(key, 4)
    noise = jax.random.normal(key, (QUERIES, IHEADS, DI), jnp.float32)
    values = noise
    return jnp.clip(values, -100.0, 100.0).astype(jnp.bfloat16)


def draw_idx_weight(key, part):
    key = jax.random.fold_in(key, 5)
    values = 0.5 * jax.random.normal(key, (QUERIES, IHEADS), jnp.float32)
    return jnp.clip(values, -1.5, 1.5).astype(jnp.bfloat16)


def shuffle_order(subkey):
    return jax.random.permutation(subkey, CONTEXT // BLK).astype(jnp.int32)


def draw_sel_blocks(key, part):
    key = jax.random.fold_in(key, 7)
    row_count = QUERIES // BLK
    total_block_count = CONTEXT // BLK
    owner_blocks = KEY_DEV // BLK
    ranking_permute = jax.vmap(shuffle_order)(jax.random.split(key, row_count))
    strongest_blocks = jax.random.randint(jax.random.fold_in(key, 1), (), 0, N_CTX - 1)
    blocks_all = jnp.arange(total_block_count, dtype=jnp.int32)
    diagonal = total_block_count - row_count + jnp.arange(row_count, dtype=jnp.int32)
    holder_lookup = blocks_all // owner_blocks
    causal = blocks_all[None, :] <= diagonal[:, None]
    grouped = jnp.where(causal, ranking_permute, -1).reshape(row_count, N_CTX, owner_blocks)
    larger = jnp.sum((grouped[:, :, None, :] > grouped[:, :, :, None]).astype(jnp.int32), axis=-1)
    permitted_mask = causal & (larger.reshape(row_count, total_block_count) < CAP)
    extra_reward = jnp.where(holder_lookup[None, :] == strongest_blocks, total_block_count, 0)
    closing_scores = jnp.where(permitted_mask, ranking_permute + extra_reward, -1)
    unused, picked = lax.top_k(closing_scores, SEL)
    return picked.astype(jnp.int32)


def setup_inputs(seed: int = 0) -> dict:
    key_list = jax.random.split(jax.random.key(seed), 7)
    latents = draw_latents(jax.random.fold_in(key_list[6], 71), 0)
    idx_keys = draw_idx_keys(jax.random.fold_in(key_list[6], 71), 0)
    mla_query = draw_mla_query(jax.random.fold_in(key_list[6], 71), 0)
    idx_query = draw_idx_query(jax.random.fold_in(key_list[6], 71), 0)
    idx_weight = draw_idx_weight(jax.random.fold_in(key_list[6], 71), 0)
    sel_blocks = draw_sel_blocks(jax.random.fold_in(key_list[6], 71), 0)
    return dict(latents=latents, idx_keys=idx_keys, mla_query=mla_query, idx_query=idx_query, idx_weight=idx_weight, sel_blocks=sel_blocks)


MLA_SCALE = 192.0 ** -0.5
FLOOR_SCORE = -1.0e30


def finish(target, logits, visible, span_keys):
    masked = jnp.where(visible, logits, FLOOR_SCORE)
    shifted = masked - jnp.max(masked, axis=-1, keepdims=True)
    log_norm = jnp.log(jnp.sum(jnp.exp(shifted), axis=-1, keepdims=True))
    log_ratio = shifted - log_norm
    predicted = jnp.where(visible, jnp.exp(log_ratio), 0.0)
    positive = target > 0.0
    entropy = jnp.sum(jnp.where(positive, target * jnp.log(jnp.where(positive, target, 1.0)), 0.0), axis=-1)
    cross_term = jnp.sum(jnp.where(visible, target * log_ratio, 0.0), axis=-1)
    divergence = entropy - cross_term
    gradient = jnp.where(visible, span_keys * (predicted - target), 0.0).astype(jnp.bfloat16)
    return divergence, gradient


def reference(latents, idx_keys, mla_query, idx_query, idx_weight, sel_blocks):
    total_block_count = CONTEXT // BLK
    span_keys = SEL * BLK
    index_scale = DI ** -0.5
    lat_table = latents.reshape(total_block_count, BLK * LAT)
    key_table = idx_keys.reshape(total_block_count, BLK * DI)
    offsets = jnp.arange(BLK, dtype=jnp.int32)

    def block_step(running, block_row):
        chosen = sel_blocks[block_row]
        lat_rows = jnp.take(lat_table, chosen, axis=0).reshape(span_keys, LAT).astype(jnp.float32)
        key_rows = jnp.take(key_table, chosen, axis=0).reshape(span_keys, DI).astype(jnp.float32)
        first_row = block_row * BLK
        queries = lax.dynamic_slice_in_dim(mla_query, first_row, BLK, 0).astype(jnp.float32)
        index_query = lax.dynamic_slice_in_dim(idx_query, first_row, BLK, 0).astype(jnp.float32)
        weights = lax.dynamic_slice_in_dim(idx_weight, first_row, BLK, 0).astype(jnp.float32)
        key_pos = (chosen[:, None] * BLK + offsets[None, :]).reshape(span_keys)
        query_pos = CONTEXT - QUERIES + first_row + offsets
        visible = key_pos[None, :] <= query_pos[:, None]
        scores = jnp.einsum("qhl,kl->qhk", queries, lat_rows) * MLA_SCALE
        scores = jnp.where(visible[:, None, :], scores, FLOOR_SCORE)
        raised = jnp.exp(scores - jnp.max(scores, axis=-1, keepdims=True))
        chances = raised / jnp.sum(raised, axis=-1, keepdims=True)
        target = jnp.sum(chances, axis=1) / HEADS
        dots = jnp.einsum("qjd,kd->qjk", index_query, key_rows) * index_scale
        active = jnp.maximum(dots, 0.0)
        logits = jnp.sum(weights[:, :, None] * active, axis=1)
        divergence, gradient = finish(target, logits, visible, span_keys)
        grad_f = gradient.astype(jnp.float32)
        weight_grad = jnp.sum(grad_f[:, None, :] * active, axis=2)
        factor = (grad_f[:, None, :] * weights[:, :, None] * jnp.where(dots > 0.0, index_scale, 0.0)).astype(jnp.bfloat16)
        factor_f = factor.astype(jnp.float32)
        query_grad = jnp.einsum("qjk,kd->qjd", factor_f, key_rows)
        key_grad = jnp.einsum("qjk,qjd->kd", factor_f, index_query)
        running = running.at[chosen].add(key_grad.reshape(SEL, BLK * DI))
        return running, (divergence, weight_grad, query_grad)

    start = jnp.zeros((total_block_count, BLK * DI), jnp.float32)
    rows_all = jnp.arange(QUERIES // BLK, dtype=jnp.int32)
    running, (divergence, weight_grad, query_grad) = lax.scan(block_step, start, rows_all)
    kl = divergence.reshape(QUERIES)
    grad_query = query_grad.reshape(QUERIES, IHEADS, DI)
    grad_weight = weight_grad.reshape(QUERIES, IHEADS)
    grad_keys = running.reshape(total_block_count, BLK, DI)
    return (kl, grad_query, grad_weight, grad_keys)
```

```python
import functools
import math

import jax
import jax.numpy as jnp
from jax import lax
from jax.experimental import pallas as pl
from jax.experimental.pallas import tpu as pltpu
from jax.sharding import PartitionSpec as P

MESH = pl.DeviceIdType.MESH
LAT, DI, BLK, SEL = 576, 128, 64, 32
HEADS = 128
NZ, SIDE = 8, 4
NCOL = SIDE * SIDE
NCTX = 2 * NCOL
CONTEXT, QUERIES = 131072, 4096
SPAN = SEL * BLK
EXT = 640
WIDE = EXT + DI
FLOOR = -1e30
LOW = -2e30
BIG = 1 << 28
EXP_SCALE = 192.0**-0.5 * math.log2(math.e)
IDX_SCALE = DI**-0.5
UROWS = 512
F32, BF16, I32 = jnp.float32, jnp.bfloat16, jnp.int32

OFFSETS = [(0, 0)] + sorted(
    [(i // SIDE, i % SIDE) for i in range(1, NCOL)], key=lambda o: -((o[0] == 2) + (o[1] == 2))
)
CODES = [dy * SIDE + dx for dy, dx in OFFSETS]


def pick(index, values):
    out = values[0]
    for i in range(1, len(values)):
        out = jnp.where(index == i, values[i], out)
    return out


def nt(a, b):
    return lax.dot_general(a, b, (((1,), (1,)), ((), ())), preferred_element_type=F32)


def kernel(
    sel_in, lat_hbm, ik_hbm, mq_hbm, iq_hbm, iw_in,
    gk_out, gq_out, gw_out, kl_out,
    lat, ikv, selall, tbl, tbs, stage, rs, qbuf, qx, prob, mrun, zrun, mchunk, wts, xbuf,
    iq, iqt, iw, wcol, ikc, kpos, tq, tqb, tsib, tfar, fac, gwacc, gkf, gsend, grecv, kz, kr, kc,
    pm, pr, gqm, gqr, klm, klr,
    ld_s, sel_s, sel_r, tb_s, q_s, q_r, iq_s, iq_r, iw_s, iw_r, st_s, st_r, fw_s, fw_r,
    ts_s, ts_r, tf_s, tf_r, gs_s, gs_r, kz_s, kz_r, pm_s, pm_r, gq_s, gq_r, kl_s, kl_r,
):
    me = lax.axis_index("ctx")
    z = lax.axis_index("head")
    k, core = me // 2, me % 2
    ky, kx = k // SIDE, k % SIDE
    sib = 2 * k + 1 - core
    rho = z % 4
    half = z // 4
    src_ctx = 2 * k + rho // 2
    blk_b = rho % 2
    t_own = 2 * half + core

    def column(code, sign):
        dy, dx = code // SIDE, code % SIDE
        return ((ky + sign * dy + SIDE) % SIDE) * SIDE + (kx + sign * dx + SIDE) % SIDE

    def send(src, dst, ssem, rsem, ctx, head):
        own = jnp.logical_and(ctx == me, head == z)
        remote = pltpu.make_async_remote_copy(
            src, dst, ssem, rsem, device_id={"ctx": ctx, "head": head}, device_id_type=MESH
        )

        @pl.when(own)
        def _():
            pltpu.make_async_copy(src, dst, rsem).start()

        @pl.when(jnp.logical_not(own))
        def _():
            remote.start()

        def finish():
            @pl.when(jnp.logical_not(own))
            def _():
                remote.wait_send()

        return finish

    def remote(src, dst, ssem, rsem, ctx, head):
        return pltpu.make_async_remote_copy(
            src, dst, ssem, rsem, device_id={"ctx": ctx, "head": head}, device_id_type=MESH
        )

    def arrived(dst, rsem):
        pltpu.make_async_copy(dst, dst, rsem).wait()

    pending = []

    load_lat = pltpu.make_async_copy(lat_hbm, lat, ld_s.at[0])
    load_ik = pltpu.make_async_copy(ik_hbm, ikv, ld_s.at[1])
    load_lat.start()
    load_ik.start()
    barrier = pltpu.get_barrier_semaphore()

    def greet_plane(d, carry):
        pl.semaphore_signal(
            barrier, inc=1, device_id={"ctx": (me + d) % NCTX, "head": z}, device_id_type=MESH
        )
        return carry

    def greet_column(d, carry):
        for c in range(2):
            pl.semaphore_signal(
                barrier, inc=1, device_id={"ctx": 2 * k + c, "head": (z + d) % NZ}, device_id_type=MESH
            )
        return carry

    lax.fori_loop(1, NCTX, greet_plane, 0)
    lax.fori_loop(1, NZ, greet_column, 0)
    selall[pl.ds(me, 1), 0:2, 0:SEL] = sel_in[...].reshape(1, 2, SEL)
    pl.semaphore_wait(barrier, NCTX - 1 + 2 * (NZ - 1))

    def sel_copy(d):
        return remote(
            selall.at[me], selall.at[me], sel_s.at[d], sel_r.at[me], (me + d) % NCTX, z
        )

    def sel_start(d, carry):
        sel_copy(d).start()
        return carry

    lax.fori_loop(1, NCTX, sel_start, 0)

    for b in range(2):
        r = 2 * core + b
        d = (r - z + 8) % 4
        for hq in range(2):
            dz = pick(d, [0, 1, 2, 7] if hq == 0 else [0, 1, 6, 7])
            tcore = pick(d, [0, 0, 0, 1] if hq == 0 else [1, 0, 1, 1])
            unit = pick(d, [0, 1, 3, 1] if hq == 0 else [0, 2, 3, 2])
            pending.append(
                send(
                    mq_hbm.at[pl.ds(BLK * b + 32 * hq, 32)], qbuf.at[unit],
                    q_s.at[2 * b + hq], q_r.at[unit], 2 * k + tcore, (z + dz) % NZ,
                )
            )
    for b in range(2):
        for t in range(4):
            tz = 2 * core + b + 4 * (t // 2)
            tc = 2 * k + t % 2
            pending.append(
                send(
                    iq_hbm.at[pl.ds((BLK * b + 16 * t) * 8, 128)], iq.at[z],
                    iq_s.at[4 * b + t], iq_r.at[z], tc, tz,
                )
            )
            pending.append(
                send(
                    iw_in.at[pl.ds(BLK * b + 16 * t, 16)], iw.at[z],
                    iw_s.at[4 * b + t], iw_r.at[z], tc, tz,
                )
            )

    def sel_wait(d, carry):
        src = (me + d) % NCTX
        arrived(selall.at[src], sel_r.at[src])
        return carry

    lax.fori_loop(1, NCTX, sel_wait, 0)
    lane = lax.broadcasted_iota(I32, (NCTX, 128), 1)
    sub = lax.broadcasted_iota(I32, (NCTX, 128), 0)
    lane_f = lane.astype(F32)
    sub3 = lax.broadcasted_iota(I32, (NCTX, 8, 128), 1)

    def rows_of(b):
        return jnp.sum(jnp.where(sub3 == b, selall[...], 0).astype(F32), axis=1).astype(I32)

    def two(match, values):
        first = jnp.min(jnp.where(match, lane_f, 128.0), axis=1, keepdims=True)
        hit0 = jnp.logical_and(match, lane_f == first)
        hit1 = jnp.logical_and(match, lane_f > first)
        second = jnp.min(jnp.where(hit1, lane_f, 128.0), axis=1, keepdims=True)
        v0 = jnp.sum(jnp.where(hit0, values, 0.0), axis=1, keepdims=True)
        v1 = jnp.sum(jnp.where(hit1, values, 0.0), axis=1, keepdims=True)
        return first, second, v0, v1

    def lanes(columns):
        out = jnp.zeros((NCTX, 128), F32)
        for i, c in enumerate(columns):
            out = jnp.where(lane == i, c, out)
        return out

    listed = lane < SEL
    wanted = []
    for b in range(2):
        rows = rows_of(b)
        match = jnp.logical_and(listed, rows // BLK == me)
        _, _, v0, v1 = two(match, (rows % BLK + 1).astype(F32))
        wanted += [v0 - 1.0, v1 - 1.0]
    table1 = lanes(wanted)
    tbl[0:NCTX, :] = table1.astype(I32)

    sub8 = lax.broadcasted_iota(I32, (8, 128), 0)

    def row_of(ctx, b):
        tile = selall[pl.ds(ctx, 1)].reshape(8, 128)
        return jnp.sum(jnp.where(sub8 == b, tile, 0).astype(F32), axis=0, keepdims=True)

    def by_owner(row):
        row = jnp.broadcast_to(row.astype(I32), (NCTX, 128))
        match = jnp.logical_and(listed, row // BLK == sub)
        return match, two(match, row.astype(F32) + 1.0)

    my_row = row_of(src_ctx, blk_b)
    match, (first, second, v0, v1) = by_owner(my_row)
    base0 = jnp.where(v0 > 0.5, (v0 - 1.0) * BLK, float(BIG))
    base1 = jnp.where(v1 > 0.5, (v1 - 1.0) * BLK, float(BIG))
    owner_col = sub // 2
    code = ((ky - owner_col // SIDE + SIDE) % SIDE) * SIDE + (kx - owner_col % SIDE + SIDE) % SIDE
    place = jnp.zeros_like(code)
    for i, c in enumerate(CODES):
        place = jnp.where(code == c, i, place)
    slot = (place * 4 + (sub % 2) * 2).astype(F32) + jnp.where(lane_f == first, 0.0, 1.0)
    slots = jnp.sum(jnp.where(match, slot, 0.0), axis=0, keepdims=True)
    columns = [base0, base1]
    for b in range(2):
        _, (f, s, _, _) = by_owner(row_of(me, b))
        columns += [jnp.minimum(f, float(SEL)), jnp.minimum(s, float(SEL))]
    tbl[NCTX : 2 * NCTX, :] = lanes(columns).astype(I32)
    tbl[2 * NCTX : 2 * NCTX + 8, :] = jnp.where(
        sub8 == 0, jnp.broadcast_to(slots, (8, 128)), jnp.broadcast_to(my_row, (8, 128))
    ).astype(I32)
    to_smem = pltpu.make_async_copy(tbl, tbs, tb_s.at[0])
    to_smem.start()
    to_smem.wait()
    load_lat.wait()
    load_ik.wait()

    def gather(code, put):
        ctx = 2 * column(code, 1) + rho // 2
        for r in range(2):
            index = jnp.clip(tbs[ctx, 2 * blk_b + r], 0, BLK - 1)
            rows = lat[pl.ds(index, 1)].reshape(BLK, LAT)
            tail = jnp.concatenate(
                [rows[:, 512:LAT], jnp.zeros((BLK, EXT - LAT), BF16)], axis=1
            )
            put(r, rows[:, 0:512], tail, ikv[pl.ds(index, 1)].reshape(BLK, DI))

    def put_own(r, head, tail, keys):
        rs[0, core, r, :, 0:512] = head
        rs[0, core, r, :, 512:EXT] = tail
        rs[0, core, r, :, EXT:WIDE] = keys

    def stage_copy(i):
        to = 2 * column(pick(i, CODES), 1) + core
        return remote(stage.at[i], rs.at[i, core], st_s.at[i], st_r.at[i], to, z)

    def stage_send(i, carry):
        def put(r, head, tail, keys):
            stage[i, r, :, 0:512] = head
            stage[i, r, :, 512:EXT] = tail
            stage[i, r, :, EXT:WIDE] = keys

        gather(pick(i, CODES), put)
        stage_copy(i).start()
        return carry

    lax.fori_loop(1, NCOL, stage_send, 0)
    gather(0, put_own)

    def forward_copy(i):
        return remote(rs.at[i, core], rs.at[i, core], fw_s.at[i], fw_r.at[i], sib, z)

    key_off = lax.broadcasted_iota(I32, (BLK, 128), 0)
    lane_q = lax.broadcasted_iota(I32, (BLK, 128), 1)
    q_base = CONTEXT - QUERIES + src_ctx * 128 + blk_b * BLK
    reach = lane_q - BLK + q_base - key_off

    def forward(c):
        for e in range(2):
            i = 2 * c + e

            @pl.when(i > 0)
            def _():
                arrived(rs.at[i, core], st_r.at[i])

            forward_copy(i).start()

    def settle(c):
        for e in range(2):
            i = 2 * c + e
            arrived(rs.at[i, 1 - core], fw_r.at[i])
            forward_copy(i).wait_send()
            owner_k = column(pick(i, CODES), -1)
            for oc in range(2):
                for r in range(2):
                    base = tbs[NCTX + 2 * owner_k + oc, r]
                    old = rs[i, oc, r, :, 512:EXT].astype(F32)
                    bias = jnp.where(base > reach, FLOOR, 0.0)
                    rs[i, oc, r, :, 512:EXT] = jnp.where(lane_q < BLK, old, bias).astype(BF16)

    def query_unit(u):
        arrived(qbuf.at[u], q_r.at[u])
        v = qbuf[u].reshape(UROWS, LAT)
        first_q = pick(u, [32 * core, 0, 32, 32 * core])
        row = lax.broadcasted_iota(I32, (UROWS, 64), 0) // 16 + first_q
        col = lax.broadcasted_iota(I32, (UROWS, 64), 1)
        hot = jnp.where(row == col, 1.0, 0.0).astype(BF16)
        qx[u, :, 0:512] = v[:, 0:512]
        qx[u, :, 512:EXT] = jnp.concatenate([v[:, 512:LAT], hot], axis=1)
        mrun[u] = jnp.full((1, UROWS), LOW, F32)
        zrun[u] = jnp.zeros((1, UROWS), F32)

    def pair(u, c):
        keys = rs[pl.ds(2 * c, 2), :, :, :, 0:EXT].reshape(512, EXT)
        s = nt(keys, qx[u])
        old = mrun[u]
        new = jnp.maximum(old, jnp.max(s, axis=0, keepdims=True))
        p = jnp.exp2((s - new) * EXP_SCALE)
        zrun[u] = zrun[u] * jnp.exp2((old - new) * EXP_SCALE) + jnp.sum(p, axis=0, keepdims=True)
        mrun[u] = new
        mchunk[c, u] = new
        prob[c, u] = p.astype(BF16).reshape(8, BLK, UROWS)

    def pairs(us, cs):
        n = len(us)
        u0, c0 = us[0], cs[0]

        def step(i, carry):
            pair(u0 + i % n, c0 + i // n)
            return carry

        lax.fori_loop(0, n * len(cs), step, 0)

    def chunks(us, first_c, last_c):
        def step(c, carry):
            forward(c)

            def inner(u, carry2):
                pair(u, c - 1)
                return carry2

            lax.fori_loop(us[0], us[-1] + 1, inner, 0)
            settle(c)
            return carry

        lax.fori_loop(first_c, last_c, step, 0)

    query_unit(0)
    forward(0)
    settle(0)
    chunks([0], 1, 4)
    for u in (1, 2):
        query_unit(u)
    pairs([1, 2], [0, 1, 2])
    chunks([0, 1, 2], 4, 6)
    query_unit(3)
    pairs([3], [0, 1, 2, 3, 4])
    chunks([0, 1, 2, 3], 6, 8)
    pairs([0, 1, 2, 3], [7])

    for u in range(4):
        scale = 1.0 / (zrun[u] * HEADS)
        for c in range(8):
            wts[c, u] = jnp.exp2((mchunk[c, u] - mrun[u]) * EXP_SCALE) * scale

    def compact(i, carry):
        s = jnp.clip(tbs[2 * NCTX, i], 0, 63)
        c, j = s // 8, s % 8

        def part(u):
            return prob[pl.ds(c, 1), pl.ds(u, 1), pl.ds(j, 1)].reshape(BLK, UROWS).astype(F32) * wts[
                pl.ds(c, 1), pl.ds(u, 1)
            ].reshape(1, UROWS)

        xbuf[0, pl.ds(i, 1)] = (part(0) + part(3) + part(1 + core)).astype(BF16).reshape(1, BLK, UROWS)
        xbuf[1, pl.ds(i, 1)] = part(2 - core).astype(BF16).reshape(1, BLK, UROWS)
        ikc[pl.ds(i, 1)] = rs[
            pl.ds(s // 4, 1), pl.ds(s // 2 % 2, 1), pl.ds(s % 2, 1), :, EXT:WIDE
        ].reshape(1, BLK, DI)
        return carry

    lax.fori_loop(0, SEL, compact, 0)
    fold = jnp.where(
        lax.broadcasted_iota(I32, (32, UROWS), 0) == lax.broadcasted_iota(I32, (32, UROWS), 1) // 16, 1.0, 0.0
    ).astype(BF16)
    for x in range(2):
        part = nt(fold, xbuf[x].reshape(SPAN, UROWS))
        h = core if x == 0 else 1 - core
        tq[pl.ds(2 * h, 2)] = part.reshape(2, 16, SPAN)
        tqb[pl.ds(2 * h, 2)] = part.astype(BF16).reshape(2, 16, SPAN)
    sib_copies = [
        remote(tqb.at[1 - core + 2 * h], tsib.at[h], ts_s.at[h], ts_r.at[h], sib, z) for h in range(2)
    ]
    for copy in sib_copies:
        copy.start()

    row_q = lax.broadcasted_iota(I32, (128, 16), 0) // 8
    spread = jnp.where(row_q == lax.broadcasted_iota(I32, (128, 16), 1), 1.0, 0.0).astype(BF16)
    row_j = lax.broadcasted_iota(I32, (128, 8), 0) % 8
    for s in range(NZ):
        arrived(iq.at[s], iq_r.at[s])
        arrived(iw.at[s], iw_r.at[s])
        w = jnp.dot(spread, iw[s], preferred_element_type=F32)
        w = jnp.sum(
            jnp.where(row_j == lax.broadcasted_iota(I32, (128, 8), 1), w, 0.0), axis=1, keepdims=True
        )
        wcol[s] = jnp.broadcast_to(w * IDX_SCALE, (128, 128))
        iqt[:, 128 * s : 128 * (s + 1)] = iq[s].astype(F32).T.astype(BF16)

    TILE = 512

    def dots_of(s, kt):
        keys = ikc[pl.ds(kt * (TILE // BLK), TILE // BLK)].reshape(TILE, DI)
        return nt(iq[s], keys)

    logit_tiles = []
    for kt in range(SPAN // TILE):
        acc = jnp.zeros((128, TILE), F32)
        for s in range(NZ):
            w = jnp.concatenate([wcol[s]] * (TILE // 128), axis=1)
            acc = acc + w * jnp.maximum(dots_of(s, kt), 0.0)
        logit_tiles.append(jnp.sum(acc.reshape(16, 8, TILE), axis=1))
    logits = jnp.concatenate(logit_tiles, axis=1)

    def positions(i, carry):
        l8 = lax.broadcasted_iota(I32, (8, 128), 1)
        a, b = tbs[2 * NCTX + 1, 2 * i] * BLK, tbs[2 * NCTX + 1, 2 * i + 1] * BLK
        kpos[pl.ds(i, 1)] = (jnp.where(l8 < BLK, a, b) + l8 % BLK).reshape(1, 8, 128)
        return carry

    lax.fori_loop(0, SPAN // 128, positions, 0)
    q_pos = q_base + 16 * t_own + lax.broadcasted_iota(I32, (16, 128), 0)
    visible = jnp.concatenate(
        [jnp.concatenate([kpos[i]] * 2, axis=0) <= q_pos for i in range(SPAN // 128)], axis=1
    )

    for h, copy in enumerate(sib_copies):
        arrived(tsib.at[h], ts_r.at[h])
        copy.wait_send()
    far = 1 - half
    mine = tq[pl.ds(2 * half + core, 1)].reshape(16, SPAN) + tsib[pl.ds(half, 1)].reshape(16, SPAN).astype(F32)
    other = tq[pl.ds(2 * far + core, 1)].reshape(16, SPAN) + tsib[pl.ds(far, 1)].reshape(16, SPAN).astype(F32)
    tfar[0] = other.astype(BF16)
    far_copy = remote(tfar.at[0], tfar.at[1], tf_s.at[0], tf_r.at[0], me, (z + 4) % NZ)
    far_copy.start()
    masked = jnp.where(visible, logits, FLOOR)
    shifted = masked - jnp.max(masked, axis=1, keepdims=True)
    log_norm = jnp.log(jnp.sum(jnp.exp(shifted), axis=1, keepdims=True))
    log_ratio = shifted - log_norm
    predicted = jnp.where(visible, jnp.exp(log_ratio), 0.0)
    arrived(tfar.at[1], tf_r.at[0])
    target = mine + tfar[1].astype(F32)
    positive = target > 0.0
    entropy = jnp.sum(
        jnp.where(positive, target * jnp.log(jnp.where(positive, target, 1.0)), 0.0), axis=1, keepdims=True
    )
    cross = jnp.sum(jnp.where(visible, target * log_ratio, 0.0), axis=1, keepdims=True)
    gradient = jnp.where(visible, SPAN * (predicted - target), 0.0).astype(BF16).astype(F32)
    divergence = entropy - cross
    spot = lax.broadcasted_iota(I32, (16, 128), 0) == lax.broadcasted_iota(I32, (16, 128), 1)
    klm[...] = jnp.broadcast_to(
        jnp.sum(jnp.where(spot, divergence, 0.0), axis=0, keepdims=True), (8, 128)
    )
    pending.append(
        send(klm, klr, kl_s.at[0], kl_r.at[0], src_ctx, 4 * blk_b + t_own)
    )

    for kt in range(SPAN // TILE):
        g = gradient[:, kt * TILE : (kt + 1) * TILE]
        g = jnp.broadcast_to(g.reshape(16, 1, TILE), (16, 8, TILE)).reshape(128, TILE)
        for s in range(NZ):
            dots = dots_of(s, kt)
            weighted = g * jnp.maximum(dots, 0.0)
            lanesum = weighted[:, 0:128]
            for i in range(1, TILE // 128):
                lanesum = lanesum + weighted[:, 128 * i : 128 * (i + 1)]
            gwacc[s] = lanesum if kt == 0 else gwacc[s] + lanesum
            w = jnp.concatenate([wcol[s]] * (TILE // 128), axis=1)
            fac[128 * s : 128 * (s + 1), kt * TILE : (kt + 1) * TILE] = jnp.where(
                dots > 0.0, g * w, 0.0
            ).astype(BF16)
    unspread = jnp.where(
        lax.broadcasted_iota(I32, (16, 128), 0) == lax.broadcasted_iota(I32, (16, 128), 1) // 8, 1.0, 0.0
    )
    diag_j = lax.broadcasted_iota(I32, (128, 128), 0) % 8 == lax.broadcasted_iota(I32, (128, 128), 1)
    for s in range(NZ):
        gq = jnp.dot(
            fac[128 * s : 128 * (s + 1), :], ikc[...].reshape(SPAN, DI), preferred_element_type=F32
        )
        gqm[s, 0:128, :] = gq.astype(BF16)
        gw = jnp.sum(gwacc[s], axis=1, keepdims=True) * IDX_SCALE
        gw = jnp.dot(
            unspread, jnp.where(diag_j, gw, 0.0), preferred_element_type=F32, precision=lax.Precision.HIGHEST
        )
        gqm[s, 128:144, :] = gw.astype(BF16)
        pending.append(
            send(
                gqm.at[s], gqr.at[4 * blk_b + t_own], gq_s.at[s], gq_r.at[4 * blk_b + t_own], src_ctx, s
            )
        )
    for kt in range(SPAN // TILE):
        part = jnp.dot(
            iqt[...], fac[:, kt * TILE : (kt + 1) * TILE], preferred_element_type=F32
        )
        gkf[kt * (TILE // BLK) : (kt + 1) * (TILE // BLK)] = part.T.reshape(TILE // BLK, BLK, DI)

    gsend[...] = gkf[:, pl.ds(32 * (1 - core), 32), :].astype(BF16)
    swap = remote(gsend, grecv, gs_s.at[0], gs_r.at[0], sib, z)
    swap.start()
    arrived(grecv, gs_r.at[0])
    both = gkf[:, pl.ds(32 * core, 32), :] + grecv[...].astype(F32)
    for t in range(4):
        kz[t] = both[:, 8 * t : 8 * t + 8, :].reshape(SEL * 8, DI).astype(BF16)
        pending.append(
            send(
                kz.at[t], kr.at[2 * blk_b + half], kz_s.at[t], kz_r.at[2 * blk_b + half],
                src_ctx, 4 * core + t,
            )
        )
    swap.wait_send()
    for b in range(2):
        for h in range(2):
            arrived(kr.at[2 * b + h], kz_r.at[2 * b + h])
        total = kr[2 * b].astype(F32) + kr[2 * b + 1].astype(F32)
        kc[b, 0:SEL] = total.reshape(SEL, 8, DI)
        kc[b, SEL : SEL + 1] = jnp.zeros((1, 8, DI), F32)

    def owner_copy(o):
        return remote(pm.at[o], pr.at[me], pm_s.at[o], pm_r.at[me], o, z)

    def owner_block(o):
        parts = []
        for b in range(2):
            for r in range(2):
                index = jnp.clip(tbs[NCTX + o, 2 + 2 * b + r], 0, SEL)
                parts.append(kc[pl.ds(b, 1), pl.ds(index, 1)].reshape(8, DI))
        return jnp.concatenate(parts, axis=0).astype(BF16)

    def owner_of(i):
        return 2 * column(pick(i // 2, CODES), 1) + (core + i) % 2

    def owner_send(i, carry):
        o = owner_of(i)
        pm[pl.ds(o, 1)] = owner_block(o).reshape(1, 32, DI)
        owner_copy(o).start()
        return carry

    lax.fori_loop(1, NCTX, owner_send, 0)
    pr[pl.ds(me, 1)] = owner_block(me).reshape(1, 32, DI)

    col = lax.broadcasted_iota(I32, (128, 1024), 1)
    expand = jnp.where(col % 32 // 8 == lax.broadcasted_iota(I32, (128, 1024), 0), 1.0, 0.0).astype(BF16)
    wide = jnp.dot(table1.astype(BF16), expand, preferred_element_type=F32)
    col = lax.broadcasted_iota(I32, (NCTX, 1024), 1)
    wide = jnp.where(col // 32 == lax.broadcasted_iota(I32, (NCTX, 1024), 0), wide * 8.0, 0.0)
    code = jnp.sum(wide, axis=0, keepdims=True) + (
        lax.broadcasted_iota(I32, (1, 1024), 1) % 8
    ).astype(F32)
    row = lax.broadcasted_iota(I32, (512, 1024), 0).astype(F32)
    hot = jnp.where(row == code, 1.0, 0.0).astype(BF16)

    arrived(klr, kl_r.at[0])
    kl_out[...] = klr[0:1, :]
    for i in range(8):
        arrived(gqr.at[i], gq_r.at[i])
        gq_out[128 * i : 128 * (i + 1), :] = gqr[i, 0:128, :].astype(F32)
        gw_out[16 * i : 16 * (i + 1), :] = gqr[i, 128:144, 0:8].astype(F32)

    def owner_wait(i, carry):
        o = owner_of(i)
        arrived(pr.at[o], pm_r.at[o])
        owner_copy(o).wait_send()
        return carry

    lax.fori_loop(1, NCTX, owner_wait, 0)
    gk_out[...] = jnp.dot(hot, pr[...].reshape(1024, DI), preferred_element_type=F32)

    for finish in pending:
        finish()
    far_copy.wait_send()

    def drain_sel(d, carry):
        sel_copy(d).wait_send()
        return carry

    def drain_stage(i, carry):
        stage_copy(i).wait_send()
        return carry

    lax.fori_loop(1, NCTX, drain_sel, 0)
    lax.fori_loop(1, NCOL, drain_stage, 0)


def local(latents, idx_keys, mla_query, idx_query, idx_weight, sel_blocks):
    V = pltpu.VMEM
    dma = pltpu.SemaphoreType.DMA
    hbm = pl.BlockSpec(memory_space=pl.ANY)
    vmem = pl.BlockSpec(memory_space=pltpu.VMEM)
    scratch = [
        V((BLK, BLK, LAT), BF16), V((BLK, BLK, DI), BF16), V((NCTX, 8, 128), I32),
        V((2 * NCTX + 8, 128), I32), pltpu.SMEM((2 * NCTX + 8, 128), I32),
        V((NCOL, 2, BLK, WIDE), BF16), V((NCOL, 2, 2, BLK, WIDE), BF16),
        V((4, 32, 16, LAT), BF16), V((4, UROWS, EXT), BF16),
        V((8, 4, 8, BLK, UROWS), BF16), V((4, 1, UROWS), F32), V((4, 1, UROWS), F32),
        V((8, 4, 1, UROWS), F32), V((8, 4, 1, UROWS), F32), V((2, SEL, BLK, UROWS), BF16),
        V((NZ, 128, DI), BF16), V((DI, NZ * 128), BF16), V((NZ, 16, 8), BF16), V((NZ, 128, 128), F32),
        V((SEL, BLK, DI), BF16), V((SPAN // 128, 8, 128), I32),
        V((4, 16, SPAN), F32), V((4, 16, SPAN), BF16), V((2, 16, SPAN), BF16), V((2, 16, SPAN), BF16),
        V((NZ * 128, SPAN), BF16), V((NZ, 128, 128), F32), V((SEL, BLK, DI), F32),
        V((SEL, 32, DI), BF16), V((SEL, 32, DI), BF16),
        V((4, SEL * 8, DI), BF16), V((4, SEL * 8, DI), BF16), V((2, SEL + 1, 8, DI), F32),
        V((NCTX, 32, DI), BF16), V((NCTX, 32, DI), BF16),
        V((NZ, 144, DI), BF16), V((8, 144, DI), BF16), V((8, 128), F32), V((8, 128), F32),
        dma((2,)), dma((NCTX,)), dma((NCTX,)), dma((1,)),
        dma((4,)), dma((4,)), dma((8,)), dma((8,)), dma((8,)), dma((8,)),
        dma((NCOL,)), dma((NCOL,)), dma((NCOL,)), dma((NCOL,)),
        dma((2,)), dma((2,)), dma((1,)), dma((1,)), dma((1,)), dma((1,)),
        dma((4,)), dma((4,)), dma((NCTX,)), dma((NCTX,)), dma((8,)), dma((8,)), dma((1,)), dma((1,)),
    ]
    gk, gq, gw, kl = pl.pallas_call(
        kernel,
        out_shape=[
            jax.ShapeDtypeStruct((BLK * 8, DI), F32),
            jax.ShapeDtypeStruct((128 * 8, DI), F32),
            jax.ShapeDtypeStruct((128, 8), F32),
            jax.ShapeDtypeStruct((1, 128), F32),
        ],
        in_specs=[vmem, hbm, hbm, hbm, hbm, vmem],
        out_specs=[vmem] * 4,
        scratch_shapes=scratch,
        compiler_params=pltpu.CompilerParams(
            collective_id=0, has_side_effects=True, vmem_limit_bytes=62 * 1024 * 1024
        ),
        name="indexer_step",
    )(
        sel_blocks,
        latents.reshape(BLK, BLK, LAT),
        idx_keys.reshape(BLK, BLK, DI),
        mla_query,
        idx_query.reshape(128 * 8, DI),
        idx_weight,
    )
    return kl[0, 0:16], gq.reshape(128, 8, DI), gw, gk.reshape(BLK, 8, DI)


def solution(mesh):
    in_specs = (
        P("ctx", None),
        P("ctx", None),
        P("ctx", "head", None),
        P("ctx", "head", None),
        P("ctx", "head"),
        P("ctx", None),
    )
    out_specs = (
        P(("ctx", "head")),
        P("ctx", "head", None),
        P("ctx", "head"),
        P("ctx", "head", None),
    )
    return jax.shard_map(local, mesh=mesh, in_specs=in_specs, out_specs=out_specs, check_vma=False)
```

```python
import functools
import math

import jax
import jax.numpy as jnp
from jax import lax
from jax.experimental import pallas as pl
from jax.experimental.pallas import tpu as pltpu
from jax.sharding import PartitionSpec as P

MESH = pl.DeviceIdType.MESH
LAT, DI, BLK, SEL = 576, 128, 64, 32
HEADS = 128
NZ, SIDE = 8, 4
NCOL = SIDE * SIDE
NCTX = 2 * NCOL
CONTEXT, QUERIES = 131072, 4096
SPAN = SEL * BLK
EXT = 640
WIDE = EXT + DI
FLOOR = -1e30
LOW = -2e30
EXP_SCALE = 192.0**-0.5 * math.log2(math.e)
IDX_SCALE = DI**-0.5
UROWS = 512
F32, BF16, I32 = jnp.float32, jnp.bfloat16, jnp.int32

OFFSETS = [(0, 0)] + sorted(
    [(i // SIDE, i % SIDE) for i in range(1, NCOL)], key=lambda o: -((o[0] == 2) + (o[1] == 2))
)
CODES = [dy * SIDE + dx for dy, dx in OFFSETS]


def pick(index, values):
    out = values[0]
    for i in range(1, len(values)):
        out = jnp.where(index == i, values[i], out)
    return out


def nt(a, b):
    return lax.dot_general(a, b, (((1,), (1,)), ((), ())), preferred_element_type=F32)


def kernel(
    sel_in, lat_hbm, ik_hbm, mq_hbm, iq_hbm, iw_in,
    gk_out, gq_out, kl_out,
    lat, ikv, selall, tbl, tbs, tbl1, tbs1, stage, rs, held, kbuf, qt, qbuf, qx, prob, mrun, zrun, mchunk, wts, xbuf, xs,
    iq, iqt, iwf, iw, wcol, ikc, kpos, tq, tqb, tsib, tfar, gwacc, gkf, gsend, grecv, kz, kr, kc,
    pm, pr, gqm, gqr, klm, klr,
    ld_s, lq_s, li_s, sel_s, sel_r, tb_s, q_s, q_r, iq_s, iq_r, iw_s, iw_r, st_s, st_r, fw_s, fw_r,
    ts_s, ts_r, tf_s, tf_r, gs_s, gs_r, kz_s, kz_r, pm_s, pm_r, gq_s, gq_r, kl_s, kl_r,
):
    me = lax.axis_index("ctx")
    z = lax.axis_index("head")
    k, core = me // 2, me % 2
    ky, kx = k // SIDE, k % SIDE
    sib = 2 * k + 1 - core
    rho = z % 4
    half = z // 4
    src_ctx = 2 * k + rho // 2
    blk_b = rho % 2
    t_own = 2 * half + core

    def column(code, sign, c):
        dy, dx = code // SIDE, code % SIDE
        sign = sign * (1 - 2 * c)
        return ((ky + sign * dy + SIDE) % SIDE) * SIDE + (kx + sign * dx + SIDE) % SIDE

    def send(src, dst, ssem, rsem, ctx, head):
        own = jnp.logical_and(ctx == me, head == z)
        remote = pltpu.make_async_remote_copy(
            src, dst, ssem, rsem, device_id={"ctx": ctx, "head": head}, device_id_type=MESH
        )

        @pl.when(own)
        def _():
            pltpu.make_async_copy(src, dst, rsem).start()

        @pl.when(jnp.logical_not(own))
        def _():
            remote.start()

        def finish():
            @pl.when(jnp.logical_not(own))
            def _():
                remote.wait_send()

        return finish

    def send_parts(src, dst, ssem, rsem, ctx, head, early):
        own = jnp.logical_and(ctx == me, head == z)
        away = jnp.logical_not(own)
        copy = remote(src, dst, ssem, rsem, ctx, head)

        def first():
            @pl.when(own)
            def _():
                pltpu.make_async_copy(src, dst, rsem).start()

            @pl.when(jnp.logical_and(away, early))
            def _():
                copy.start()

        def second():
            @pl.when(jnp.logical_and(away, jnp.logical_not(early)))
            def _():
                copy.start()

        def done():
            @pl.when(away)
            def _():
                copy.wait_send()

        return first, second, done

    def remote(src, dst, ssem, rsem, ctx, head):
        return pltpu.make_async_remote_copy(
            src, dst, ssem, rsem, device_id={"ctx": ctx, "head": head}, device_id_type=MESH
        )

    def arrived(dst, rsem):
        pltpu.make_async_copy(dst, dst, rsem).wait()

    pending = []

    def load_query(h):
        return pltpu.make_async_copy(
            mq_hbm.at[h],
            xbuf.at[h // 8, pl.ds(9 * (h // 4 % 2), 9), :, pl.ds(pl.multiple_of(h % 4 * 128, 128), 128)],
            lq_s.at[h],
        )

    def load_latents(n):
        return pltpu.make_async_copy(
            lat_hbm.at[:, :, pl.ds(pl.multiple_of(n * 128, 128), 128)], lat.at[n], ld_s.at[n]
        )

    load_ik = pltpu.make_async_copy(ik_hbm, ikv, li_s.at[0])
    for h in range(16):
        load_query(h).start()

    def start_latents(n, carry):
        load_latents(n).start()
        return carry

    lax.fori_loop(0, BLK // 2, start_latents, 0)
    load_ik.start()
    barrier = pltpu.get_barrier_semaphore()

    def greet_plane(d, carry):
        pl.semaphore_signal(
            barrier, inc=1, device_id={"ctx": (me + d) % NCTX, "head": z}, device_id_type=MESH
        )
        return carry

    def greet_column(d, carry):
        for c in range(2):
            pl.semaphore_signal(
                barrier, inc=1, device_id={"ctx": 2 * k + c, "head": (z + d) % NZ}, device_id_type=MESH
            )
        return carry

    lax.fori_loop(1, NCTX, greet_plane, 0)
    lax.fori_loop(1, NZ, greet_column, 0)
    selall[pl.ds(me, 1), 0:2, 0:SEL] = sel_in[...].reshape(1, 2, SEL)
    iwf[...] = iw_in[...].astype(F32)

    def turn_query(h, carry):
        tails = []
        for e in range(2):
            hh = h + 8 * e
            load_query(hh).wait()
            raw = xbuf.at[e, pl.ds(9 * (h // 4), 9), :, pl.ds(pl.multiple_of(h % 4 * 128, 128), 128)][...]
            rows = raw[0:8].reshape(512, 128).T
            for n in range(4):
                for t in range(4):
                    qt[n, pl.ds(16 * t + hh, 1)] = rows[32 * n : 32 * n + 32, 128 * t : 128 * t + 128].reshape(
                        1, 32, 128
                    )
            tails.append(raw[8])
        tail = jnp.concatenate(tails, axis=0).T
        for n in range(4):
            qt[n, pl.ds(64 + h, 1)] = tail[32 * n : 32 * n + 32, :].reshape(1, 32, 128)
        return carry

    lax.fori_loop(0, 8, turn_query, 0)
    pl.semaphore_wait(barrier, NCTX - 1 + 2 * (NZ - 1))

    def sel_copy(d):
        return remote(
            selall.at[me], selall.at[me], sel_s.at[d], sel_r.at[me], (me + d) % NCTX, z
        )

    def sel_start(d, carry):
        sel_copy(d).start()
        return carry

    lax.fori_loop(1, NCTX, sel_start, 0)

    far_sends = []
    for b in range(2):
        r = 2 * core + b
        d = (r - z + 8) % 4
        for hq in range(2):
            dz = pick(d, [0, 1, 2, 7] if hq == 0 else [0, 1, 6, 7])
            tcore = pick(d, [0, 0, 0, 1] if hq == 0 else [1, 0, 1, 1])
            unit = pick(d, [0, 1, 3, 1] if hq == 0 else [0, 2, 3, 2])
            first, second, done = send_parts(
                qt.at[2 * b + hq], qbuf.at[unit],
                q_s.at[2 * b + hq], q_r.at[unit], 2 * k + tcore, (z + dz) % NZ, d != 2,
            )
            first()
            far_sends.append(second)
            pending.append(done)
    for second in far_sends:
        second()

    def sel_wait(d, carry):
        src = (me + d) % NCTX
        arrived(selall.at[src], sel_r.at[src])
        return carry

    lax.fori_loop(1, NCTX, sel_wait, 0)
    lane = lax.broadcasted_iota(I32, (NCTX, 128), 1)
    sub = lax.broadcasted_iota(I32, (NCTX, 128), 0)
    lane_f = lane.astype(F32)
    sub3 = lax.broadcasted_iota(I32, (NCTX, 8, 128), 1)

    def rows_of(b):
        return jnp.sum(jnp.where(sub3 == b, selall[...], 0).astype(F32), axis=1).astype(I32)

    def two(match, values):
        first = jnp.min(jnp.where(match, lane_f, 128.0), axis=1, keepdims=True)
        hit0 = jnp.logical_and(match, lane_f == first)
        hit1 = jnp.logical_and(match, lane_f > first)
        v0 = jnp.sum(jnp.where(hit0, values, 0.0), axis=1, keepdims=True)
        v1 = jnp.sum(jnp.where(hit1, values, 0.0), axis=1, keepdims=True)
        return v0, v1

    def lanes(columns):
        out = jnp.zeros((NCTX, 128), F32)
        for i, c in enumerate(columns):
            out = jnp.where(lane == i, c, out)
        return out

    listed = lane < SEL
    wanted = []
    for b in range(2):
        rows = rows_of(b)
        match = jnp.logical_and(listed, rows // BLK == me)
        v0, v1 = two(match, (rows % BLK + 1).astype(F32))
        wanted += [v0 - 1.0, v1 - 1.0]
    table1 = lanes(wanted)
    tbl1[...] = table1.astype(I32)
    to_smem1 = pltpu.make_async_copy(tbl1, tbs1, tb_s.at[1])
    to_smem1.start()

    to_smem1.wait()
    load_ik.wait()

    def wait_latents(n, carry):
        load_latents(n).wait()
        return carry

    lax.fori_loop(0, BLK // 2, wait_latents, 0)

    lane_b = lax.broadcasted_iota(I32, (BLK, 128), 1)

    def gather(code, into):
        ctx = 2 * column(code, 1, core) + rho // 2
        tails, odds = [], []
        for r in range(2):
            index = jnp.clip(tbs1[ctx, 2 * blk_b + r], 0, BLK - 1)
            odd = index % 2 == 1
            raw = lat[pl.ds(index // 2, 1)].reshape(9, BLK, 128)
            rows = raw[0:8].reshape(512, 128).T
            rows = jnp.where(odd, rows[BLK:, :], rows[:BLK, :])
            for t in range(4):
                into[4 * r + t] = rows[:, 128 * t : 128 * t + 128]
            tails.append(raw[8])
            odds.append(odd)
            into[9 + r] = ikv[pl.ds(index, 1)].reshape(BLK, DI)
        tail = jnp.concatenate(tails, axis=0).T.astype(F32)
        tails = [jnp.where(odd, tail[BLK:, :], tail[:BLK, :]) for odd in odds]
        into[8] = jnp.where(lane_b < BLK, tails[0], tails[1]).astype(BF16)

    def stage_copy(i):
        to = 2 * column(pick(i, CODES), 1, core) + core
        return remote(stage.at[i], rs.at[i, core], st_s.at[i], st_r.at[i], to, z)

    def stage_send(i, carry):
        gather(pick(i, CODES), stage.at[i])
        stage_copy(i).start()
        return carry

    lax.fori_loop(1, NCOL, stage_send, 0)
    for b in range(2):
        for t in range(4):
            tz = 2 * core + b + 4 * (t // 2)
            tc = 2 * k + t % 2
            pending.append(
                send(
                    iq_hbm.at[pl.ds((BLK * b + 16 * t) * 8, 128)], iq.at[z],
                    iq_s.at[4 * b + t], iq_r.at[z], tc, tz,
                )
            )
            pending.append(
                send(iwf, iw.at[z], iw_s.at[4 * b + t], iw_r.at[z], tc, tz)
            )
    gather(0, rs.at[0, core])

    sub8 = lax.broadcasted_iota(I32, (8, 128), 0)

    def row_of(ctx, b):
        tile = selall[pl.ds(ctx, 1)].reshape(8, 128)
        return jnp.sum(jnp.where(sub8 == b, tile, 0).astype(F32), axis=0, keepdims=True)

    def by_owner(row):
        row = jnp.broadcast_to(row.astype(I32), (NCTX, 128))
        match = jnp.logical_and(listed, row // BLK == sub)
        return two(match, row.astype(F32) + 1.0)

    def use_order(col_index, odd):
        dy = ky - col_index // SIDE
        dx = kx - col_index % SIDE
        dy, dx = jnp.where(odd, -dy, dy), jnp.where(odd, -dx, dx)
        code = ((dy + SIDE) % SIDE) * SIDE + (dx + SIDE) % SIDE
        place = jnp.zeros_like(code)
        for i, c in enumerate(CODES):
            place = jnp.where(code == c, i, place)
        return place * 2 + odd.astype(I32)

    order = use_order(sub // 2, sub % 2 == 1)
    order_lane = use_order(lane % NCTX // 2, lane % 2 == 1)
    before = jnp.where(jnp.logical_and(order_lane < order, lane < NCTX), 1.0, 0.0)[:, 0:NCTX].astype(BF16)

    def number(row):
        v0, v1 = by_owner(row)
        has0, has1 = v0 > 0.5, v1 > 0.5
        count = jnp.where(has0, 1.0, 0.0) + jnp.where(has1, 1.0, 0.0)
        count = jnp.broadcast_to(count, (NCTX, 128)).astype(BF16)
        n0 = jnp.dot(before, count, preferred_element_type=F32)
        return v0, v1, jnp.where(has0, n0, float(SEL)), jnp.where(has1, n0 + 1.0, float(SEL))

    v0, v1, n0, n1 = number(row_of(src_ctx, blk_b))
    hit0 = jnp.logical_and(lane_f == n0, listed)
    hit1 = jnp.logical_and(lane_f == n1, listed)
    slot = order.astype(F32) * 2.0

    def along(a, b):
        total = jnp.where(hit0, a, 0.0) + jnp.where(hit1, b, 0.0)
        return jnp.sum(total, axis=0, keepdims=True)

    slots = along(slot, slot + 1.0)
    blocks = along(v0 - 1.0, v1 - 1.0)
    columns = [v0, v1]
    for b in range(2):
        _, _, m0, m1 = number(row_of(me, b))
        columns += [m0, m1]
    tbl[0:NCTX, :] = lanes(columns).astype(I32)
    tbl[NCTX : NCTX + 8, :] = jnp.where(
        sub8 == 0, jnp.broadcast_to(slots, (8, 128)), jnp.broadcast_to(blocks, (8, 128))
    ).astype(I32)
    to_smem = pltpu.make_async_copy(tbl, tbs, tb_s.at[0])
    to_smem.start()
    to_smem.wait()

    def forward_copy(i):
        return remote(rs.at[i, core], rs.at[i, core], fw_s.at[i], fw_r.at[i], sib, z)

    key_off = lax.broadcasted_iota(I32, (BLK, 128), 0)
    q_base = CONTEXT - QUERIES + src_ctx * 128 + blk_b * BLK
    reach = lane_b - BLK + q_base - key_off

    def forward(c):
        for e in range(2):
            i = 2 * c + e

            @pl.when(i > 0)
            def _():
                arrived(rs.at[i, core], st_r.at[i])

            forward_copy(i).start()

    def settle(c):
        for e in range(2):
            i = 2 * c + e
            arrived(rs.at[i, 1 - core], fw_r.at[i])
            held[pl.ds(i, 1)] = rs[pl.ds(i, 1)]

    def collect(g):
        def block(j, carry):
            n = 8 * g + j
            s = jnp.clip(tbs[NCTX, n], 0, 63)
            odd = s % 2 == 1
            place = held.at[pl.ds(s // 4, 1), pl.ds(s // 2 % 2, 1)]
            at = pl.ds(pl.multiple_of(j * BLK, BLK), BLK)
            for t in range(4):
                kbuf[g, at, 128 * t : 128 * t + 128] = place[:, :, pl.ds(s % 2 * 4 + t, 1)].reshape(BLK, 128)
            tail = place[:, :, 8].reshape(BLK, 128).astype(F32)
            tail = jnp.where(odd, pltpu.roll(tail, 64, 1), tail)
            bias = jnp.where(tbs[NCTX + 1, n] * BLK > reach, FLOOR, 0.0)
            kbuf[g, at, 512:EXT] = jnp.where(lane_b < BLK, tail, bias).astype(BF16)
            ikc[pl.ds(n, 1)] = place[:, :, pl.ds(9 + s % 2, 1)].reshape(1, BLK, DI)
            return carry

        lax.fori_loop(0, 8, block, 0)

    def query_unit(u):
        arrived(qbuf.at[u], q_r.at[u])
        first_q = pick(u, [32 * core, 0, 32, 32 * core])
        row = lax.broadcasted_iota(I32, (256, 128), 0) % 32 + first_q
        col = lax.broadcasted_iota(I32, (256, 128), 1)
        hot = jnp.where(row == col - BLK, 1.0, 0.0)
        for t in range(4):
            qx[u, :, 128 * t : 128 * t + 128] = qbuf[u, 16 * t : 16 * t + 16].reshape(UROWS, 128)
        tail = qbuf[u, 64:72].reshape(256, 128).astype(F32)
        qx[u, 0:256, 512:EXT] = jnp.where(col < BLK, tail, hot).astype(BF16)
        qx[u, 256:512, 512:EXT] = jnp.where(col < BLK, pltpu.roll(tail, 64, 1), hot).astype(BF16)
        mrun[u] = jnp.full((1, UROWS), LOW, F32)
        zrun[u] = jnp.zeros((1, UROWS), F32)

    def pair(u, c):
        keys = kbuf[c]
        parts = [nt(keys, qx[u, 256 * h : 256 * h + 256, :]) for h in range(2)]
        for h in range(2):
            s = parts[h]
            lanes_h = slice(256 * h, 256 * h + 256)
            old = mrun[u, :, lanes_h]
            new = jnp.maximum(old, jnp.max(s, axis=0, keepdims=True))
            p = jnp.exp2((s - new) * EXP_SCALE)
            zrun[u, :, lanes_h] = zrun[u, :, lanes_h] * jnp.exp2((old - new) * EXP_SCALE) + jnp.sum(
                p, axis=0, keepdims=True
            )
            mrun[u, :, lanes_h] = new
            mchunk[c, u, :, lanes_h] = new
            prob[c, pl.ds(8 * u, 8), :, lanes_h] = p.astype(BF16).reshape(8, BLK, 256)

    def group(g):
        collect(g)

        def step(u, carry):
            pair(u, g)
            return carry

        lax.fori_loop(0, 4, step, 0)

    def step(c, carry):
        forward(c)

        @pl.when(c > 0)
        def _():
            settle(c - 1)

        return carry

    lax.fori_loop(0, 6, step, 0)
    for u in range(4):
        query_unit(u)
    group(0)
    step(6, 0)
    group(1)
    own_q = lax.broadcasted_iota(I32, (128, 128), 0) // 8 + BLK * blk_b + 16 * t_own
    own_q = own_q == lax.broadcasted_iota(I32, (128, 128), 1)
    for s in range(NZ):
        arrived(iq.at[s], iq_r.at[s])
        arrived(iw.at[s], iw_r.at[s])
        w = jnp.broadcast_to(iw[s].reshape(1, 8, 128), (16, 8, 128)).reshape(128, 128)
        w = jnp.sum(jnp.where(own_q, w, 0.0), axis=1, keepdims=True)
        wcol[s] = jnp.broadcast_to(w * IDX_SCALE, (128, 128))
        iqt[:, 128 * s : 128 * (s + 1)] = iq[s].astype(F32).T.astype(BF16)

    step(7, 0)
    group(2)
    settle(7)
    group(3)

    for u in range(4):
        scale = 1.0 / (zrun[u] * HEADS)
        for c in range(4):
            w = jnp.exp2((mchunk[c, u] - mrun[u]) * EXP_SCALE) * scale
            wts[c, u] = jnp.broadcast_to(w, (16, UROWS)).astype(BF16)

    def compact(i, carry):
        c, j = i // 8, i % 8

        def part(u):
            p = prob[pl.ds(c, 1), pl.ds(8 * u + j, 1)].reshape(4, 16, UROWS)
            return p * wts[pl.ds(c, 1), pl.ds(u, 1)].reshape(1, 16, UROWS)

        def narrow(p):
            p = p.reshape(BLK, UROWS).astype(F32)
            p = (p[:, 0:128] + p[:, 128:256]) + (p[:, 256:384] + p[:, 384:512])
            return p.astype(BF16).reshape(1, BLK, 128)

        xs[0, pl.ds(i, 1)] = narrow(part(0) + part(3) + part(1 + core))
        xs[1, pl.ds(i, 1)] = narrow(part(2 - core))
        return carry

    lax.fori_loop(0, SEL, compact, 0)
    fold = jnp.where(
        lax.broadcasted_iota(I32, (32, 128), 0) == lax.broadcasted_iota(I32, (32, 128), 1) % 32, 1.0, 0.0
    ).astype(BF16)
    for x in range(2):
        part = nt(fold, xs[x].reshape(SPAN, 128))
        h = core if x == 0 else 1 - core
        tq[pl.ds(2 * h, 2)] = part.reshape(2, 16, SPAN)
        tqb[pl.ds(2 * h, 2)] = part.astype(BF16).reshape(2, 16, SPAN)
    sib_copies = [
        remote(tqb.at[1 - core + 2 * h], tsib.at[h], ts_s.at[h], ts_r.at[h], sib, z) for h in range(2)
    ]
    for copy in sib_copies:
        copy.start()

    TILE = 512

    def dots_of(s, kt):
        keys = ikc[pl.ds(kt * (TILE // BLK), TILE // BLK)].reshape(TILE, DI)
        return nt(iq[s], keys)

    def logit_tile(kt):
        acc = jnp.zeros((128, TILE), F32)
        for s in range(NZ):
            w = jnp.concatenate([wcol[s]] * (TILE // 128), axis=1)
            acc = acc + w * jnp.maximum(dots_of(s, kt), 0.0)
        return jnp.sum(acc.reshape(16, 8, TILE), axis=1)

    logit_tiles = [logit_tile(0)]

    def positions(i, carry):
        l8 = lax.broadcasted_iota(I32, (8, 128), 1)
        a, b = tbs[NCTX + 1, 2 * i] * BLK, tbs[NCTX + 1, 2 * i + 1] * BLK
        kpos[pl.ds(i, 1)] = (jnp.where(l8 < BLK, a, b) + l8 % BLK).reshape(1, 8, 128)
        return carry

    lax.fori_loop(0, SPAN // 128, positions, 0)
    q_pos = q_base + 16 * t_own + lax.broadcasted_iota(I32, (16, 128), 0)
    visible = jnp.concatenate(
        [jnp.concatenate([kpos[i]] * 2, axis=0) <= q_pos for i in range(SPAN // 128)], axis=1
    )

    for h, copy in enumerate(sib_copies):
        arrived(tsib.at[h], ts_r.at[h])
        copy.wait_send()
    far = 1 - half
    mine = tq[pl.ds(2 * half + core, 1)].reshape(16, SPAN) + tsib[pl.ds(half, 1)].reshape(16, SPAN).astype(F32)
    other = tq[pl.ds(2 * far + core, 1)].reshape(16, SPAN) + tsib[pl.ds(far, 1)].reshape(16, SPAN).astype(F32)
    tfar[0] = other.astype(BF16)
    far_copy = remote(tfar.at[0], tfar.at[1], tf_s.at[0], tf_r.at[0], me, (z + 4) % NZ)
    far_copy.start()
    logit_tiles += [logit_tile(kt) for kt in range(1, SPAN // TILE)]
    logits = jnp.concatenate(logit_tiles, axis=1)
    masked = jnp.where(visible, logits, FLOOR)
    shifted = masked - jnp.max(masked, axis=1, keepdims=True)
    log_norm = jnp.log(jnp.sum(jnp.exp(shifted), axis=1, keepdims=True))
    log_ratio = shifted - log_norm
    predicted = jnp.where(visible, jnp.exp(log_ratio), 0.0)
    arrived(tfar.at[1], tf_r.at[0])
    target = mine + tfar[1].astype(F32)
    positive = target > 0.0
    entropy = jnp.sum(
        jnp.where(positive, target * jnp.log(jnp.where(positive, target, 1.0)), 0.0), axis=1, keepdims=True
    )
    cross = jnp.sum(jnp.where(visible, target * log_ratio, 0.0), axis=1, keepdims=True)
    gradient = jnp.where(visible, SPAN * (predicted - target), 0.0).astype(BF16).astype(F32)
    divergence = entropy - cross
    spot = lax.broadcasted_iota(I32, (16, 128), 0) == lax.broadcasted_iota(I32, (16, 128), 1)
    klm[...] = jnp.broadcast_to(
        jnp.sum(jnp.where(spot, divergence, 0.0), axis=0, keepdims=True), (8, 128)
    )
    pending.append(
        send(klm, klr, kl_s.at[0], kl_r.at[0], src_ctx, 4 * blk_b + t_own)
    )

    KB = TILE // BLK

    def swap(kt):
        part = pl.ds(kt * KB, KB)
        return remote(gsend.at[part], grecv.at[part], gs_s.at[kt], gs_r.at[kt], sib, z)

    def cores_sum(kt):
        here = slice(kt * KB, (kt + 1) * KB)
        arrived(grecv.at[pl.ds(kt * KB, KB)], gs_r.at[kt])
        both = gkf[here, pl.ds(32 * core, 32), :] + grecv[here].astype(F32)
        to = 2 * blk_b + half
        for t in range(4):
            kz[t, kt] = both[:, 8 * t : 8 * t + 8, :].reshape(KB * 8, DI).astype(BF16)
            pending.append(
                send(
                    kz.at[t, kt], kr.at[to, kt], kz_s.at[4 * t + kt], kz_r.at[4 * to + kt],
                    src_ctx, 4 * core + t,
                )
            )

    for kt in range(SPAN // TILE):
        g = gradient[:, kt * TILE : (kt + 1) * TILE]
        g = jnp.broadcast_to(g.reshape(16, 1, TILE), (16, 8, TILE)).reshape(128, TILE)
        for s in range(NZ):
            dots = dots_of(s, kt)
            weighted = g * jnp.maximum(dots, 0.0)
            lanesum = weighted[:, 0:128]
            for i in range(1, TILE // 128):
                lanesum = lanesum + weighted[:, 128 * i : 128 * (i + 1)]
            gwacc[s] = lanesum if kt == 0 else gwacc[s] + lanesum
            w = jnp.concatenate([wcol[s]] * (TILE // 128), axis=1)
            prob[kt, 2 * s : 2 * s + 2] = (
                jnp.where(dots > 0.0, g * w, 0.0).astype(BF16).reshape(2, BLK, TILE)
            )
        part = jnp.dot(iqt[...], prob[kt, 0 : 2 * NZ].reshape(NZ * 128, TILE), preferred_element_type=F32)
        here = slice(kt * KB, (kt + 1) * KB)
        gkf[here] = part.T.reshape(KB, BLK, DI)
        gsend[here] = gkf[here, pl.ds(32 * (1 - core), 32), :].astype(BF16)
        swap(kt).start()
        if kt > 0:
            cores_sum(kt - 1)
    unspread = jnp.where(
        lax.broadcasted_iota(I32, (16, 128), 0) == lax.broadcasted_iota(I32, (16, 128), 1) // 8, 1.0, 0.0
    )
    diag_j = lax.broadcasted_iota(I32, (128, 128), 0) % 8 == lax.broadcasted_iota(I32, (128, 128), 1)
    for s in range(NZ):
        gq = jnp.dot(
            jnp.concatenate(
                [prob[kt, 2 * s : 2 * s + 2].reshape(128, TILE) for kt in range(SPAN // TILE)], axis=1
            ),
            ikc[...].reshape(SPAN, DI), preferred_element_type=F32
        )
        gqm[s, 0:128, :] = gq.astype(BF16)
        gw = jnp.sum(gwacc[s], axis=1, keepdims=True) * IDX_SCALE
        gw = jnp.dot(
            unspread, jnp.where(diag_j, gw, 0.0), preferred_element_type=F32, precision=lax.Precision.HIGHEST
        )
        gqm[s, 128:144, :] = gw.astype(BF16)
    cores_sum(SPAN // TILE - 1)
    for s in range(NZ):
        pending.append(
            send(
                gqm.at[s], gqr.at[4 * blk_b + t_own], gq_s.at[s], gq_r.at[4 * blk_b + t_own], src_ctx, s
            )
        )
    for kt in range(SPAN // TILE):
        swap(kt).wait_send()
    for b in range(2):
        for h in range(2):
            for kt in range(SPAN // TILE):
                arrived(kr.at[2 * b + h, kt], kz_r.at[4 * (2 * b + h) + kt])
        total = kr[2 * b].astype(F32) + kr[2 * b + 1].astype(F32)
        kc[b, 0:SEL] = total.reshape(SEL, 8, DI)
        kc[b, SEL : SEL + 1] = jnp.zeros((1, 8, DI), F32)

    def owner_copy(o):
        return remote(pm.at[o], pr.at[me], pm_s.at[o], pm_r.at[me], o, z)

    def owner_block(o):
        parts = []
        for b in range(2):
            for r in range(2):
                index = jnp.clip(tbs[o, 2 + 2 * b + r], 0, SEL)
                parts.append(kc[pl.ds(b, 1), pl.ds(index, 1)].reshape(8, DI))
        return jnp.concatenate(parts, axis=0).astype(BF16)

    def owner_of(i):
        return (me + i) % NCTX

    def owner_send(i, carry):
        o = owner_of(i)
        pm[pl.ds(o, 1)] = owner_block(o).reshape(1, 32, DI)
        owner_copy(o).start()
        return carry

    lax.fori_loop(1, NCTX, owner_send, 0)
    pr[pl.ds(me, 1)] = owner_block(me).reshape(1, 32, DI)

    col = lax.broadcasted_iota(I32, (128, 1024), 1)
    expand = jnp.where(col % 32 // 8 == lax.broadcasted_iota(I32, (128, 1024), 0), 1.0, 0.0).astype(BF16)
    wide = jnp.dot(table1.astype(BF16), expand, preferred_element_type=F32)
    col = lax.broadcasted_iota(I32, (NCTX, 1024), 1)
    wide = jnp.where(col // 32 == lax.broadcasted_iota(I32, (NCTX, 1024), 0), wide * 8.0, 0.0)
    code = jnp.sum(wide, axis=0, keepdims=True) + (
        lax.broadcasted_iota(I32, (1, 1024), 1) % 8
    ).astype(F32)
    row = lax.broadcasted_iota(I32, (512, 1024), 0).astype(F32)
    hot = jnp.where(row == code, 1.0, 0.0).astype(BF16)

    arrived(klr, kl_r.at[0])
    kl_out[...] = klr[...]
    for i in range(8):
        arrived(gqr.at[i], gq_r.at[i])
        gq_out[i] = gqr[i]

    def owner_wait(i, carry):
        o = owner_of(i)
        arrived(pr.at[o], pm_r.at[o])
        owner_copy(o).wait_send()
        return carry

    lax.fori_loop(1, NCTX, owner_wait, 0)
    gk_out[...] = jnp.dot(hot, pr[...].reshape(1024, DI), preferred_element_type=F32)

    for finish in pending:
        finish()
    far_copy.wait_send()

    def drain_sel(d, carry):
        sel_copy(d).wait_send()
        return carry

    def drain_stage(i, carry):
        stage_copy(i).wait_send()
        return carry

    lax.fori_loop(1, NCTX, drain_sel, 0)
    lax.fori_loop(1, NCOL, drain_stage, 0)

    def drain_forward(i, carry):
        forward_copy(i).wait_send()
        return carry

    lax.fori_loop(0, NCOL, drain_forward, 0)


def unpack(gk, gq, kl, gk_out, gq_out, gw_out, kl_out):
    gk_out[...] = gk[...].reshape(BLK, 8, DI)
    weights = []
    for i in range(8):
        gq_out[16 * i : 16 * (i + 1)] = gq[i, 0:128, :].astype(F32).reshape(16, 8, DI)
        weights.append(gq[i, 128:144, :].astype(F32))
    gw_out[...] = jnp.concatenate(weights, axis=0).T[0:8, :]
    kl_out[...] = kl[0, 0:16]


def local(latents, idx_keys, mla_query, idx_query, idx_weight, sel_blocks):
    V = pltpu.VMEM
    dma = pltpu.SemaphoreType.DMA
    hbm = pl.BlockSpec(memory_space=pl.ANY)
    vmem = pl.BlockSpec(memory_space=pltpu.VMEM)
    scratch = [
        V((BLK // 2, 9, BLK, 128), BF16), V((BLK, BLK, DI), BF16), V((NCTX, 8, 128), I32),
        V((NCTX + 8, 128), I32), pltpu.SMEM((NCTX + 8, 128), I32),
        V((NCTX, 128), I32), pltpu.SMEM((NCTX, 128), I32),
        V((NCOL, 11, BLK, 128), BF16), V((NCOL, 2, 11, BLK, 128), BF16),
        V((NCOL, 2, 11, BLK, 128), BF16), V((4, 512, EXT), BF16),
        V((4, 72, 32, 128), BF16), V((4, 72, 32, 128), BF16), V((4, UROWS, EXT), BF16),
        V((4, 32, BLK, UROWS), BF16), V((4, 1, UROWS), F32), V((4, 1, UROWS), F32),
        V((4, 4, 1, UROWS), F32), V((4, 4, 16, UROWS), BF16),
        V((2, SEL, BLK, UROWS), BF16), V((2, SEL, BLK, 128), BF16),
        V((NZ, 128, DI), BF16), V((DI, NZ * 128), BF16),
        V((8, 128), F32), V((NZ, 8, 128), F32), V((NZ, 128, 128), F32),
        V((SEL, BLK, DI), BF16), V((SPAN // 128, 8, 128), I32),
        V((4, 16, SPAN), F32), V((4, 16, SPAN), BF16), V((2, 16, SPAN), BF16), V((2, 16, SPAN), BF16),
        V((NZ, 128, 128), F32), V((SEL, BLK, DI), F32),
        V((SEL, 32, DI), BF16), V((SEL, 32, DI), BF16),
        V((4, 4, SEL * 2, DI), BF16), V((4, 4, SEL * 2, DI), BF16), V((2, SEL + 1, 8, DI), F32),
        V((NCTX, 32, DI), BF16), V((NCTX, 32, DI), BF16),
        V((NZ, 144, DI), BF16), V((8, 144, DI), BF16), V((8, 128), F32), V((8, 128), F32),
        dma((BLK // 2,)), dma((16,)), dma((1,)), dma((NCTX,)), dma((NCTX,)), dma((2,)),
        dma((4,)), dma((4,)), dma((8,)), dma((8,)), dma((8,)), dma((8,)),
        dma((NCOL,)), dma((NCOL,)), dma((NCOL,)), dma((NCOL,)),
        dma((2,)), dma((2,)), dma((1,)), dma((1,)), dma((4,)), dma((4,)),
        dma((16,)), dma((16,)), dma((NCTX,)), dma((NCTX,)), dma((8,)), dma((8,)), dma((1,)), dma((1,)),
    ]
    gk, gq, kl = pl.pallas_call(
        kernel,
        out_shape=[
            jax.ShapeDtypeStruct((BLK * 8, DI), F32),
            jax.ShapeDtypeStruct((8, 144, DI), BF16),
            jax.ShapeDtypeStruct((8, 128), F32),
        ],
        in_specs=[vmem, hbm, hbm, hbm, hbm, vmem],
        out_specs=[vmem] * 3,
        scratch_shapes=scratch,
        compiler_params=pltpu.CompilerParams(
            collective_id=0, has_side_effects=True, vmem_limit_bytes=62 * 1024 * 1024
        ),
        name="indexer_step",
    )(
        sel_blocks,
        latents.T.reshape(9, BLK, BLK * BLK),
        idx_keys.reshape(BLK, BLK, DI),
        mla_query.transpose(1, 2, 0).reshape(16, 9, BLK, 128),
        idx_query.reshape(128 * 8, DI),
        idx_weight.T,
    )
    grad_keys, grad_query, grad_weight, divergence = pl.pallas_call(
        unpack,
        out_shape=[
            jax.ShapeDtypeStruct((BLK, 8, DI), F32),
            jax.ShapeDtypeStruct((128, 8, DI), F32),
            jax.ShapeDtypeStruct((8, 128), F32),
            jax.ShapeDtypeStruct((16,), F32),
        ],
        in_specs=[vmem] * 3,
        out_specs=[vmem] * 4,
        name="unpack",
    )(gk, gq, kl)
    return divergence, grad_query, grad_weight.T, grad_keys


def solution(mesh):
    in_specs = (
        P("ctx", None),
        P("ctx", None),
        P("ctx", "head", None),
        P("ctx", "head", None),
        P("ctx", "head"),
        P("ctx", None),
    )
    out_specs = (
        P(("ctx", "head")),
        P("ctx", "head", None),
        P("ctx", "head"),
        P("ctx", "head", None),
    )
    return jax.shard_map(local, mesh=mesh, in_specs=in_specs, out_specs=out_specs, check_vma=False)
```

```python
import functools
import math

import jax
import jax.numpy as jnp
from jax import lax
from jax.experimental import pallas as pl
from jax.experimental.pallas import tpu as pltpu
from jax.sharding import PartitionSpec as P

MESH = pl.DeviceIdType.MESH
LAT, DI, BLK, SEL = 576, 128, 64, 32
HEADS = 128
NZ, SIDE = 8, 4
NCOL = SIDE * SIDE
NCTX = 2 * NCOL
CONTEXT, QUERIES = 131072, 4096
SPAN = SEL * BLK
EXT = 640
WIDE = EXT + DI
FLOOR = -1e30
LOW = -2e30
EXP_SCALE = 192.0**-0.5 * math.log2(math.e)
IDX_SCALE = DI**-0.5
UROWS = 512
IN_FLIGHT, LAG = 5, 6
F32, BF16, I32 = jnp.float32, jnp.bfloat16, jnp.int32

OFFSETS = [(0, 0), (0, 1), (0, 3), (1, 0), (3, 0), (1, 1), (3, 3), (1, 3), (3, 1)]
OFFSETS += [(0, 2), (2, 0), (1, 2), (2, 1), (3, 2), (2, 3), (2, 2)]
CODES = [dy * SIDE + dx for dy, dx in OFFSETS]


def pick(index, values):
    out = values[0]
    for i in range(1, len(values)):
        out = jnp.where(index == i, values[i], out)
    return out


def wrap(value, n):
    return jnp.where(value >= n, value - n, value)


def nt(a, b):
    return lax.dot_general(a, b, (((1,), (1,)), ((), ())), preferred_element_type=F32)


def kernel(
    sel_in, lat_hbm, ik_hbm, mq_hbm, iq_hbm, iw_in,
    gk_out, gq_out, kl_out,
    lat, ikv, selall, tbl, tbs, tbl1, tbs1, stage, rs, held, kbuf, qt, qbuf, qx, s_even, s_odd, prob, mrun, zrun, mchunk, wts, xbuf, xs,
    iq, iqt, iwf, iw, wcol, ikc, kpos, tq, tqb, tsib, tfar, gwacc, gkf, gsend, grecv, kz, kr, kc,
    pm, pr, gqm, gqr, klm, klr, lbuf, gbuf,
    ld_s, lq_s, li_s, sel_s, sel_r, tb_s, q_s, q_r, iq_s, iq_r, iw_s, iw_r, st_s, st_r, fw_s, fw_r,
    ts_s, ts_r, tf_s, tf_r, gs_s, gs_r, kz_s, kz_r, pm_s, pm_r, gq_s, gq_r, kl_s, kl_r,
):
    me = lax.axis_index("ctx")
    z = lax.axis_index("head")
    k, core = me // 2, me % 2
    ky, kx = k // SIDE, k % SIDE
    sib = 2 * k + 1 - core
    rho = z % 4
    half = z // 4
    src_ctx = 2 * k + rho // 2
    blk_b = rho % 2
    t_own = 2 * half + core

    def column(code, sign, c):
        dy, dx = code // SIDE, code % SIDE
        sign = sign * (1 - 2 * c)
        row = wrap(wrap(ky + sign * dy + SIDE, SIDE), SIDE)
        return row * SIDE + wrap(wrap(kx + sign * dx + SIDE, SIDE), SIDE)

    class send:
        def __init__(self, src, dst, ssem, rsem, ctx, head):
            self.own = jnp.logical_and(ctx == me, head == z)
            self.here = (src, dst, rsem)
            self.away = remote(src, dst, ssem, rsem, ctx, head)

        def start(self):
            @pl.when(self.own)
            def _():
                pltpu.make_async_copy(*self.here).start()

            @pl.when(jnp.logical_not(self.own))
            def _():
                self.away.start()

        def finish(self):
            @pl.when(jnp.logical_not(self.own))
            def _():
                self.away.wait_send()

    def send_parts(src, dst, ssem, rsem, ctx, head, early):
        own = jnp.logical_and(ctx == me, head == z)
        away = jnp.logical_not(own)
        copy = remote(src, dst, ssem, rsem, ctx, head)

        def first():
            @pl.when(own)
            def _():
                pltpu.make_async_copy(src, dst, rsem).start()

            @pl.when(jnp.logical_and(away, early))
            def _():
                copy.start()

        def second():
            @pl.when(jnp.logical_and(away, jnp.logical_not(early)))
            def _():
                copy.start()

        def done():
            @pl.when(away)
            def _():
                copy.wait_send()

        return first, second, done

    def remote(src, dst, ssem, rsem, ctx, head):
        return pltpu.make_async_remote_copy(
            src, dst, ssem, rsem, device_id={"ctx": ctx, "head": head}, device_id_type=MESH
        )

    def arrived(dst, rsem):
        pltpu.make_async_copy(dst, dst, rsem).wait()

    pending = []

    def load_query(h):
        return pltpu.make_async_copy(
            mq_hbm.at[h],
            xbuf.at[h // 8, pl.ds(9 * (h // 4 % 2), 9), :, pl.ds(pl.multiple_of(h % 4 * 128, 128), 128)],
            lq_s.at[h],
        )

    def load_latents(n):
        return pltpu.make_async_copy(
            lat_hbm.at[:, :, pl.ds(pl.multiple_of(n * 128, 128), 128)], lat.at[n], ld_s.at[n]
        )

    load_ik = pltpu.make_async_copy(ik_hbm, ikv, li_s.at[0])
    for h in range(16):
        load_query(h).start()

    def start_latents(n, carry):
        load_latents(n).start()
        return carry

    lax.fori_loop(0, BLK // 2, start_latents, 0)
    load_ik.start()
    barrier = pltpu.get_barrier_semaphore()

    def greet_plane(d, carry):
        pl.semaphore_signal(
            barrier, inc=1, device_id={"ctx": wrap(me + d, NCTX), "head": z}, device_id_type=MESH
        )
        return carry

    def greet_column(d, carry):
        for c in range(2):
            pl.semaphore_signal(
                barrier, inc=1, device_id={"ctx": 2 * k + c, "head": wrap(z + d, NZ)}, device_id_type=MESH
            )
        return carry

    lax.fori_loop(1, NCTX, greet_plane, 0)
    lax.fori_loop(1, NZ, greet_column, 0)
    selall[pl.ds(me, 1), 0:2, 0:SEL] = sel_in[...].reshape(1, 2, SEL)
    iwf[...] = iw_in[...].astype(F32)

    def turn_query(h, carry):
        tails = []
        for e in range(2):
            hh = h + 8 * e
            load_query(hh).wait()
            raw = xbuf.at[e, pl.ds(9 * (h // 4), 9), :, pl.ds(pl.multiple_of(h % 4 * 128, 128), 128)][...]
            rows = raw[0:8].reshape(512, 128).T
            for n in range(4):
                for t in range(4):
                    qt[n, pl.ds(16 * t + hh, 1)] = rows[32 * n : 32 * n + 32, 128 * t : 128 * t + 128].reshape(
                        1, 32, 128
                    )
            tails.append(raw[8])
        tail = jnp.concatenate(tails, axis=0).T
        for n in range(4):
            qt[n, pl.ds(64 + h, 1)] = tail[32 * n : 32 * n + 32, :].reshape(1, 32, 128)
        return carry

    lax.fori_loop(0, 8, turn_query, 0)
    pl.semaphore_wait(barrier, NCTX - 1 + 2 * (NZ - 1))

    def sel_copy(d):
        return remote(
            selall.at[me], selall.at[me], sel_s.at[d], sel_r.at[me], wrap(me + d, NCTX), z
        )

    def sel_start(d, carry):
        sel_copy(d).start()
        return carry

    lax.fori_loop(1, NCTX, sel_start, 0)

    far_sends = []
    for b in range(2):
        r = 2 * core + b
        d = (r - z + 8) % 4
        for hq in range(2):
            dz = pick(d, [0, 1, 2, 7] if hq == 0 else [0, 1, 6, 7])
            tcore = pick(d, [0, 0, 0, 1] if hq == 0 else [1, 0, 1, 1])
            unit = pick(d, [0, 1, 3, 1] if hq == 0 else [0, 2, 3, 2])
            first, second, done = send_parts(
                qt.at[2 * b + hq], qbuf.at[unit],
                q_s.at[2 * b + hq], q_r.at[unit], 2 * k + tcore, wrap(z + dz, NZ), d != 2,
            )
            first()
            far_sends.append(second)
            pending.append(done)
    for second in far_sends:
        second()

    def sel_wait(d, carry):
        src = wrap(me + d, NCTX)
        arrived(selall.at[src], sel_r.at[src])
        return carry

    lax.fori_loop(1, NCTX, sel_wait, 0)
    lane = lax.broadcasted_iota(I32, (NCTX, 128), 1)
    sub = lax.broadcasted_iota(I32, (NCTX, 128), 0)
    lane_f = lane.astype(F32)
    sub3 = lax.broadcasted_iota(I32, (NCTX, 8, 128), 1)

    def rows_of(b):
        return jnp.sum(jnp.where(sub3 == b, selall[...], 0).astype(F32), axis=1).astype(I32)

    def two(match, values):
        first = jnp.min(jnp.where(match, lane_f, 128.0), axis=1, keepdims=True)
        hit0 = jnp.logical_and(match, lane_f == first)
        hit1 = jnp.logical_and(match, lane_f > first)
        v0 = jnp.sum(jnp.where(hit0, values, 0.0), axis=1, keepdims=True)
        v1 = jnp.sum(jnp.where(hit1, values, 0.0), axis=1, keepdims=True)
        return v0, v1

    def lanes(columns):
        out = jnp.zeros((NCTX, 128), F32)
        for i, c in enumerate(columns):
            out = jnp.where(lane == i, c, out)
        return out

    listed = lane < SEL
    wanted = []
    for b in range(2):
        rows = rows_of(b)
        match = jnp.logical_and(listed, rows // BLK == me)
        v0, v1 = two(match, (rows % BLK + 1).astype(F32))
        wanted += [v0 - 1.0, v1 - 1.0]
    table1 = lanes(wanted)
    tbl1[...] = table1.astype(I32)
    to_smem1 = pltpu.make_async_copy(tbl1, tbs1, tb_s.at[1])
    to_smem1.start()

    to_smem1.wait()
    load_ik.wait()

    def wait_latents(n, carry):
        load_latents(n).wait()
        return carry

    lax.fori_loop(0, BLK // 2, wait_latents, 0)

    lane_b = lax.broadcasted_iota(I32, (BLK, 128), 1)

    def gather(code, into):
        ctx = 2 * column(code, 1, core) + rho // 2
        tails, odds = [], []
        for r in range(2):
            index = jnp.clip(tbs1[ctx, 2 * blk_b + r], 0, BLK - 1)
            odd = index % 2 == 1
            raw = lat[pl.ds(index // 2, 1)].reshape(9, BLK, 128)
            rows = raw[0:8].reshape(512, 128).T
            rows = jnp.where(odd, rows[BLK:, :], rows[:BLK, :])
            for t in range(4):
                into[4 * r + t] = rows[:, 128 * t : 128 * t + 128]
            tails.append(raw[8])
            odds.append(odd)
            into[9 + r] = ikv[pl.ds(index, 1)].reshape(BLK, DI)
        tail = jnp.concatenate(tails, axis=0).T.astype(F32)
        tails = [jnp.where(odd, tail[BLK:, :], tail[:BLK, :]) for odd in odds]
        into[8] = jnp.where(lane_b < BLK, tails[0], tails[1]).astype(BF16)

    def stage_copy(i):
        to = 2 * column(pick(i, CODES), 1, core) + core
        return remote(stage.at[i], rs.at[i, core], st_s.at[i], st_r.at[i], to, z)

    def stage_send(n, carry):
        i = n % NCOL
        gather(pick(i, CODES), stage.at[i])

        @pl.when(i > 0)
        def _():
            stage_copy(i).start()

        return carry

    stage_send(NCOL, 0)
    lax.fori_loop(1, IN_FLIGHT + 1, stage_send, 0)
    for b in range(2):
        for t in range(4):
            tz = 2 * core + b + 4 * (t // 2)
            tc = 2 * k + t % 2
            for copy in (
                send(
                    iq_hbm.at[pl.ds((BLK * b + 16 * t) * 8, 128)], iq.at[z],
                    iq_s.at[4 * b + t], iq_r.at[z], tc, tz,
                ),
                send(iwf, iw.at[z], iw_s.at[4 * b + t], iw_r.at[z], tc, tz),
            ):
                copy.start()
                pending.append(copy.finish)
    rs[0, pl.ds(core, 1)] = stage[0:1]

    sub8 = lax.broadcasted_iota(I32, (8, 128), 0)

    def row_of(ctx, b):
        tile = selall[pl.ds(ctx, 1)].reshape(8, 128)
        return jnp.sum(jnp.where(sub8 == b, tile, 0).astype(F32), axis=0, keepdims=True)

    def by_owner(row):
        row = jnp.broadcast_to(row.astype(I32), (NCTX, 128))
        match = jnp.logical_and(listed, row // BLK == sub)
        return two(match, row.astype(F32) + 1.0)

    def use_order(col_index, odd):
        dy = ky - col_index // SIDE
        dx = kx - col_index % SIDE
        dy, dx = jnp.where(odd, -dy, dy), jnp.where(odd, -dx, dx)
        code = ((dy + SIDE) % SIDE) * SIDE + (dx + SIDE) % SIDE
        place = jnp.zeros_like(code)
        for i, c in enumerate(CODES):
            place = jnp.where(code == c, i, place)
        return place * 2 + odd.astype(I32)

    order = use_order(sub // 2, sub % 2 == 1)
    order_lane = use_order(lane % NCTX // 2, lane % 2 == 1)
    before = jnp.where(jnp.logical_and(order_lane < order, lane < NCTX), 1.0, 0.0)[:, 0:NCTX].astype(BF16)

    def number(row):
        v0, v1 = by_owner(row)
        has0, has1 = v0 > 0.5, v1 > 0.5
        count = jnp.where(has0, 1.0, 0.0) + jnp.where(has1, 1.0, 0.0)
        count = jnp.broadcast_to(count, (NCTX, 128)).astype(BF16)
        n0 = jnp.dot(before, count, preferred_element_type=F32)
        return v0, v1, jnp.where(has0, n0, float(SEL)), jnp.where(has1, n0 + 1.0, float(SEL))

    v0, v1, n0, n1 = number(row_of(src_ctx, blk_b))
    hit0 = jnp.logical_and(lane_f == n0, listed)
    hit1 = jnp.logical_and(lane_f == n1, listed)
    slot = order.astype(F32) * 2.0

    def along(a, b):
        total = jnp.where(hit0, a, 0.0) + jnp.where(hit1, b, 0.0)
        return jnp.sum(total, axis=0, keepdims=True)

    slots = along(slot, slot + 1.0)
    blocks = along(v0 - 1.0, v1 - 1.0)
    columns = [v0, v1]
    for b in range(2):
        _, _, m0, m1 = number(row_of(me, b))
        columns += [m0, m1]
    tbl[0:NCTX, :] = lanes(columns).astype(I32)
    tbl[NCTX : NCTX + 8, :] = jnp.where(
        sub8 == 0, jnp.broadcast_to(slots, (8, 128)), jnp.broadcast_to(blocks, (8, 128))
    ).astype(I32)
    to_smem = pltpu.make_async_copy(tbl, tbs, tb_s.at[0])
    to_smem.start()
    to_smem.wait()

    def forward_copy(i):
        return remote(rs.at[i, core], rs.at[i, core], fw_s.at[i], fw_r.at[i], sib, z)

    key_off = lax.broadcasted_iota(I32, (BLK, 128), 0)
    q_base = CONTEXT - QUERIES + src_ctx * 128 + blk_b * BLK
    reach = lane_b - BLK + q_base - key_off

    def forward(i):
        @pl.when(i > 0)
        def _():
            arrived(rs.at[i, core], st_r.at[i])

        forward_copy(i).start()

    def settle(i):
        arrived(rs.at[i, 1 - core], fw_r.at[i])
        held[pl.ds(i, 1)] = rs[pl.ds(i, 1)]

    def collect(g):
        def block(j, carry):
            n = 8 * g + j
            s = jnp.clip(tbs[NCTX, n], 0, 63)
            odd = s % 2 == 1
            place = held.at[pl.ds(s // 4, 1), pl.ds(s // 2 % 2, 1)]
            at = pl.ds(pl.multiple_of(j * BLK, BLK), BLK)
            for t in range(4):
                kbuf[g, at, 128 * t : 128 * t + 128] = place[:, :, pl.ds(s % 2 * 4 + t, 1)].reshape(BLK, 128)
            tail = place[:, :, 8].reshape(BLK, 128).astype(F32)
            tail = jnp.where(odd, pltpu.roll(tail, 64, 1), tail)
            bias = jnp.where(tbs[NCTX + 1, n] * BLK > reach, FLOOR, 0.0)
            kbuf[g, at, 512:EXT] = jnp.where(lane_b < BLK, tail, bias).astype(BF16)
            ikc[pl.ds(n, 1)] = place[:, :, pl.ds(9 + s % 2, 1)].reshape(1, BLK, DI)
            return carry

        lax.fori_loop(0, 8, block, 0)

    def query_unit(u):
        arrived(qbuf.at[u], q_r.at[u])
        first_q = pick(u, [32 * core, 0, 32, 32 * core])
        row = lax.broadcasted_iota(I32, (256, 128), 0) % 32 + first_q
        col = lax.broadcasted_iota(I32, (256, 128), 1)
        hot = jnp.where(row == col - BLK, 1.0, 0.0)
        for t in range(4):
            qx[u, :, 128 * t : 128 * t + 128] = qbuf[u, 16 * t : 16 * t + 16].reshape(UROWS, 128)
        tail = qbuf[u, 64:72].reshape(256, 128).astype(F32)
        qx[u, 0:256, 512:EXT] = jnp.where(col < BLK, tail, hot).astype(BF16)
        qx[u, 256:512, 512:EXT] = jnp.where(col < BLK, pltpu.roll(tail, 64, 1), hot).astype(BF16)
        mrun[u] = jnp.full((1, UROWS), LOW, F32)
        zrun[u] = jnp.zeros((1, UROWS), F32)

    def score(u, c, h, into):
        into[...] = nt(kbuf[c], qx[u, 256 * h : 256 * h + 256, :])

    def soften(u, c, h, held_scores):
        s = held_scores[...]
        lanes_h = slice(256 * h, 256 * h + 256)
        old = mrun[u, :, lanes_h]
        new = jnp.maximum(old, jnp.max(s, axis=0, keepdims=True))
        p = jnp.exp2((s - new) * EXP_SCALE)
        zrun[u, :, lanes_h] = zrun[u, :, lanes_h] * jnp.exp2((old - new) * EXP_SCALE) + jnp.sum(
            p, axis=0, keepdims=True
        )
        mrun[u, :, lanes_h] = new
        mchunk[c, u, :, lanes_h] = new
        prob[c, pl.ds(8 * u, 8), :, lanes_h] = p.astype(BF16).reshape(8, BLK, 256)

    def group(g):
        collect(g)

        def step(u, carry):
            score(u, g, 1, s_odd)
            soften(u, g, 0, s_even)
            score(jnp.minimum(u + 1, 3), g, 0, s_even)
            soften(u, g, 1, s_odd)
            return carry

        score(0, g, 0, s_even)
        lax.fori_loop(0, 4, step, 0)

    def flow(i, carry):
        @pl.when(i < NCOL)
        def _():
            stage_copy(i - IN_FLIGHT).wait_send()
            stage_send(i, 0)

        @pl.when(i >= LAG)
        def _():
            forward(i - LAG)

        @pl.when(i > LAG)
        def _():
            settle(i - LAG - 1)

        return carry

    def unit(u, carry):
        query_unit(u)
        return carry

    lax.fori_loop(IN_FLIGHT + 1, 14, flow, 0)
    lax.fori_loop(0, 4, unit, 0)
    def positions(i, carry):
        l8 = lax.broadcasted_iota(I32, (8, 128), 1)
        a, b = tbs[NCTX + 1, 2 * i] * BLK, tbs[NCTX + 1, 2 * i + 1] * BLK
        kpos[pl.ds(i, 1)] = (jnp.where(l8 < BLK, a, b) + l8 % BLK).reshape(1, 8, 128)
        return carry

    lax.fori_loop(0, SPAN // 128, positions, 0)
    own_q = lax.broadcasted_iota(I32, (128, 128), 0) // 8 + BLK * blk_b + 16 * t_own
    own_q = own_q == lax.broadcasted_iota(I32, (128, 128), 1)

    def prepare(s, carry):
        arrived(iq.at[s], iq_r.at[s])
        arrived(iw.at[s], iw_r.at[s])
        w = jnp.broadcast_to(iw[s].reshape(1, 8, 128), (16, 8, 128)).reshape(128, 128)
        w = jnp.sum(jnp.where(own_q, w, 0.0), axis=1, keepdims=True)
        wcol[s] = jnp.broadcast_to(w * IDX_SCALE, (128, 128))
        iqt[:, pl.ds(pl.multiple_of(128 * s, 128), 128)] = iq[s].astype(F32).T.astype(BF16)
        return carry

    lax.fori_loop(0, NZ, prepare, 0)

    lax.fori_loop(14, 10 + LAG, flow, 0)
    settle(9)

    def arrive_and_score(g, carry):
        @pl.when(g > 0)
        def _():
            settle(8 + 2 * g)
            settle(9 + 2 * g)

        @pl.when(g < 3)
        def _():
            forward(10 + 2 * g)
            forward(11 + 2 * g)

        group(g)
        return carry

    lax.fori_loop(0, 4, arrive_and_score, 0)

    for u in range(4):
        scale = 1.0 / (zrun[u] * HEADS)
        for c in range(4):
            w = jnp.exp2((mchunk[c, u] - mrun[u]) * EXP_SCALE) * scale
            wts[c, u] = jnp.broadcast_to(w, (16, UROWS)).astype(BF16)

    def compact(i, carry):
        c, j = i // 8, i % 8

        def part(u):
            p = prob[pl.ds(c, 1), pl.ds(8 * u + j, 1)].reshape(4, 16, UROWS)
            return p * wts[pl.ds(c, 1), pl.ds(u, 1)].reshape(1, 16, UROWS)

        def narrow(p):
            p = p.reshape(BLK, UROWS).astype(F32)
            p = (p[:, 0:128] + p[:, 128:256]) + (p[:, 256:384] + p[:, 384:512])
            return p.astype(BF16).reshape(1, BLK, 128)

        xs[0, pl.ds(i, 1)] = narrow(part(0) + part(3) + part(1 + core))
        xs[1, pl.ds(i, 1)] = narrow(part(2 - core))
        return carry

    lax.fori_loop(0, SEL, compact, 0)
    fold = jnp.where(
        lax.broadcasted_iota(I32, (32, 128), 0) == lax.broadcasted_iota(I32, (32, 128), 1) % 32, 1.0, 0.0
    ).astype(BF16)
    for x in range(2):
        part = nt(fold, xs[x].reshape(SPAN, 128))
        h = core if x == 0 else 1 - core
        tq[pl.ds(2 * h, 2)] = part.reshape(2, 16, SPAN)
        tqb[pl.ds(2 * h, 2)] = part.astype(BF16).reshape(2, 16, SPAN)
    sib_copies = [
        remote(tqb.at[1 - core + 2 * h], tsib.at[h], ts_s.at[h], ts_r.at[h], sib, z) for h in range(2)
    ]
    for copy in sib_copies:
        copy.start()

    TILE = 512

    def dots_of(s, kt):
        keys = ikc[pl.ds(kt * (TILE // BLK), TILE // BLK)].reshape(TILE, DI)
        return nt(iq[s], keys)

    def logit_tile(kt, carry):
        acc = jnp.zeros((128, TILE), F32)
        for s in range(NZ):
            w = jnp.concatenate([wcol[s]] * (TILE // 128), axis=1)
            acc = acc + w * jnp.maximum(dots_of(s, kt), 0.0)
        lbuf[kt] = jnp.sum(acc.reshape(16, 8, TILE), axis=1)
        return carry

    lax.fori_loop(0, SPAN // TILE, logit_tile, 0)

    q_pos = q_base + 16 * t_own + lax.broadcasted_iota(I32, (16, 128), 0)
    visible = jnp.concatenate(
        [jnp.concatenate([kpos[i]] * 2, axis=0) <= q_pos for i in range(SPAN // 128)], axis=1
    )

    for h, copy in enumerate(sib_copies):
        arrived(tsib.at[h], ts_r.at[h])
        copy.wait_send()
    far = 1 - half
    mine = tq[pl.ds(2 * half + core, 1)].reshape(16, SPAN) + tsib[pl.ds(half, 1)].reshape(16, SPAN).astype(F32)
    other = tq[pl.ds(2 * far + core, 1)].reshape(16, SPAN) + tsib[pl.ds(far, 1)].reshape(16, SPAN).astype(F32)
    tfar[0] = other.astype(BF16)
    far_copy = remote(tfar.at[0], tfar.at[1], tf_s.at[0], tf_r.at[0], me, wrap(z + 4, NZ))
    far_copy.start()

    for finish in pending:
        finish()

    def drain_sel(d, carry):
        sel_copy(d).wait_send()
        return carry

    def drain_stage(i, carry):
        stage_copy(i).wait_send()
        return carry

    def drain_forward(i, carry):
        forward_copy(i).wait_send()
        return carry

    lax.fori_loop(1, NCTX, drain_sel, 0)
    lax.fori_loop(NCOL - IN_FLIGHT, NCOL, drain_stage, 0)
    lax.fori_loop(0, NCOL, drain_forward, 0)
    logits = jnp.concatenate([lbuf[kt] for kt in range(SPAN // TILE)], axis=1)
    masked = jnp.where(visible, logits, FLOOR)
    shifted = masked - jnp.max(masked, axis=1, keepdims=True)
    log_norm = jnp.log(jnp.sum(jnp.exp(shifted), axis=1, keepdims=True))
    log_ratio = shifted - log_norm
    predicted = jnp.where(visible, jnp.exp(log_ratio), 0.0)
    arrived(tfar.at[1], tf_r.at[0])
    target = mine + tfar[1].astype(F32)
    positive = target > 0.0
    entropy = jnp.sum(
        jnp.where(positive, target * jnp.log(jnp.where(positive, target, 1.0)), 0.0), axis=1, keepdims=True
    )
    cross = jnp.sum(jnp.where(visible, target * log_ratio, 0.0), axis=1, keepdims=True)
    gradient = jnp.where(visible, SPAN * (predicted - target), 0.0).astype(BF16).astype(F32)
    divergence = entropy - cross
    spot = lax.broadcasted_iota(I32, (16, 128), 0) == lax.broadcasted_iota(I32, (16, 128), 1)
    klm[...] = jnp.broadcast_to(
        jnp.sum(jnp.where(spot, divergence, 0.0), axis=0, keepdims=True), (8, 128)
    )
    kl_send = send(klm, klr, kl_s.at[0], kl_r.at[0], src_ctx, 4 * blk_b + t_own)
    kl_send.start()

    KB = TILE // BLK

    def swap(kt):
        part = pl.ds(kt * KB, KB)
        return remote(gsend.at[part], grecv.at[part], gs_s.at[kt], gs_r.at[kt], sib, z)

    def kz_send(kt, t):
        to = 2 * blk_b + half
        return send(
            kz.at[t, kt], kr.at[to, kt], kz_s.at[4 * t + kt], kz_r.at[4 * to + kt], src_ctx, 4 * core + t
        )

    def cores_sum(kt):
        here = pl.ds(kt * KB, KB)
        arrived(grecv.at[here], gs_r.at[kt])
        both = gkf[here, pl.ds(32 * core, 32), :] + grecv[here].astype(F32)
        for t in range(4):
            kz[t, pl.ds(kt, 1)] = both[:, 8 * t : 8 * t + 8, :].reshape(1, KB * 8, DI).astype(BF16)
            kz_send(kt, t).start()

    for kt in range(SPAN // TILE):
        gbuf[kt] = gradient[:, kt * TILE : (kt + 1) * TILE]

    def backward(kt, carry):
        g = gbuf[kt]
        g = jnp.broadcast_to(g.reshape(16, 1, TILE), (16, 8, TILE)).reshape(128, TILE)
        for s in range(NZ):
            dots = dots_of(s, kt)
            weighted = g * jnp.maximum(dots, 0.0)
            lanesum = weighted[:, 0:128]
            for i in range(1, TILE // 128):
                lanesum = lanesum + weighted[:, 128 * i : 128 * (i + 1)]
            gwacc[s] = jnp.where(kt == 0, 0.0, gwacc[s]) + lanesum
            w = jnp.concatenate([wcol[s]] * (TILE // 128), axis=1)
            prob[kt, 2 * s : 2 * s + 2] = (
                jnp.where(dots > 0.0, g * w, 0.0).astype(BF16).reshape(2, BLK, TILE)
            )
        part = jnp.dot(iqt[...], prob[kt, 0 : 2 * NZ].reshape(NZ * 128, TILE), preferred_element_type=F32)
        here = pl.ds(kt * KB, KB)
        gkf[here] = part.T.reshape(KB, BLK, DI)
        gsend[here] = gkf[here, pl.ds(32 * (1 - core), 32), :].astype(BF16)
        swap(kt).start()

        @pl.when(kt > 0)
        def _():
            cores_sum(kt - 1)

        return carry

    lax.fori_loop(0, SPAN // TILE, backward, 0)

    unspread = jnp.where(
        lax.broadcasted_iota(I32, (16, 128), 0) == lax.broadcasted_iota(I32, (16, 128), 1) // 8, 1.0, 0.0
    )
    diag_j = lax.broadcasted_iota(I32, (128, 128), 0) % 8 == lax.broadcasted_iota(I32, (128, 128), 1)
    def query_grad(s, carry):
        factor = jnp.concatenate(
            [prob[kt, pl.ds(2 * s, 2)].reshape(128, TILE) for kt in range(SPAN // TILE)], axis=1
        )
        gq = jnp.dot(factor, ikc[...].reshape(SPAN, DI), preferred_element_type=F32)
        gw = jnp.sum(gwacc[s], axis=1, keepdims=True) * IDX_SCALE
        gw = jnp.dot(
            unspread, jnp.where(diag_j, gw, 0.0), preferred_element_type=F32, precision=lax.Precision.HIGHEST
        )
        gqm[pl.ds(s, 1), 0:128, :] = gq.astype(BF16).reshape(1, 128, DI)
        gqm[pl.ds(s, 1), 128:144, :] = gw.astype(BF16).reshape(1, 16, DI)
        return carry

    lax.fori_loop(0, NZ, query_grad, 0)
    cores_sum(SPAN // TILE - 1)

    def gq_send(s):
        return send(gqm.at[s], gqr.at[4 * blk_b + t_own], gq_s.at[s], gq_r.at[4 * blk_b + t_own], src_ctx, s)

    def gq_start(s, carry):
        gq_send(s).start()
        return carry

    lax.fori_loop(0, NZ, gq_start, 0)
    for kt in range(SPAN // TILE):
        swap(kt).wait_send()
    for b in range(2):
        for h in range(2):
            for kt in range(SPAN // TILE):
                arrived(kr.at[2 * b + h, kt], kz_r.at[4 * (2 * b + h) + kt])
        total = kr[2 * b].astype(F32) + kr[2 * b + 1].astype(F32)
        kc[b, 0:SEL] = total.reshape(SEL, 8, DI)
        kc[b, SEL : SEL + 1] = jnp.zeros((1, 8, DI), F32)

    def owner_copy(o):
        return remote(pm.at[o], pr.at[me], pm_s.at[o], pm_r.at[me], o, z)

    def owner_block(o):
        parts = []
        for b in range(2):
            for r in range(2):
                index = jnp.clip(tbs[o, 2 + 2 * b + r], 0, SEL)
                parts.append(kc[pl.ds(b, 1), pl.ds(index, 1)].reshape(8, DI))
        return jnp.concatenate(parts, axis=0).astype(BF16)

    def owner_of(i):
        return wrap(me + i, NCTX)

    def owner_send(i, carry):
        o = owner_of(i)
        pm[pl.ds(o, 1)] = owner_block(o).reshape(1, 32, DI)
        owner_copy(o).start()
        return carry

    lax.fori_loop(1, NCTX, owner_send, 0)
    pr[pl.ds(me, 1)] = owner_block(me).reshape(1, 32, DI)

    col = lax.broadcasted_iota(I32, (128, 1024), 1)
    expand = jnp.where(col % 32 // 8 == lax.broadcasted_iota(I32, (128, 1024), 0), 1.0, 0.0).astype(BF16)
    wide = jnp.dot(table1.astype(BF16), expand, preferred_element_type=F32)
    col = lax.broadcasted_iota(I32, (NCTX, 1024), 1)
    wide = jnp.where(col // 32 == lax.broadcasted_iota(I32, (NCTX, 1024), 0), wide * 8.0, 0.0)
    code = jnp.sum(wide, axis=0, keepdims=True) + (
        lax.broadcasted_iota(I32, (1, 1024), 1) % 8
    ).astype(F32)
    row = lax.broadcasted_iota(I32, (128, 1024), 0).astype(F32)

    def sum_blocks(i, carry):
        hot = jnp.where(row == code - (128 * i).astype(F32), 1.0, 0.0).astype(BF16)
        gk_out[pl.ds(pl.multiple_of(128 * i, 128), 128), :] = jnp.dot(
            hot, pr[...].reshape(1024, DI), preferred_element_type=F32
        )
        return carry


    arrived(klr, kl_r.at[0])
    kl_out[...] = klr[...]
    for i in range(8):
        arrived(gqr.at[i], gq_r.at[i])
        gq_out[i] = gqr[i]

    def owner_wait(i, carry):
        o = owner_of(i)
        arrived(pr.at[o], pm_r.at[o])
        owner_copy(o).wait_send()
        return carry

    lax.fori_loop(1, NCTX, owner_wait, 0)
    lax.fori_loop(0, 4, sum_blocks, 0)

    kl_send.finish()
    far_copy.wait_send()

    def drain_gradients(s, carry):
        gq_send(s).finish()
        for t in range(2):
            kz_send(s % 4, s // 4 * 2 + t).finish()
        return carry

    lax.fori_loop(0, NZ, drain_gradients, 0)


def unpack(gk, gq, kl, gk_out, gq_out, gw_out, kl_out):
    gk_out[...] = gk[...].reshape(BLK, 8, DI)
    weights = []
    for i in range(8):
        gq_out[16 * i : 16 * (i + 1)] = gq[i, 0:128, :].astype(F32).reshape(16, 8, DI)
        weights.append(gq[i, 128:144, :].astype(F32))
    gw_out[...] = jnp.concatenate(weights, axis=0).T[0:8, :]
    kl_out[...] = kl[0, 0:16]


def local(latents, idx_keys, mla_query, idx_query, idx_weight, sel_blocks):
    V = pltpu.VMEM
    dma = pltpu.SemaphoreType.DMA
    hbm = pl.BlockSpec(memory_space=pl.ANY)
    vmem = pl.BlockSpec(memory_space=pltpu.VMEM)
    scratch = [
        V((BLK // 2, 9, BLK, 128), BF16), V((BLK, BLK, DI), BF16), V((NCTX, 8, 128), I32),
        V((NCTX + 8, 128), I32), pltpu.SMEM((NCTX + 8, 128), I32),
        V((NCTX, 128), I32), pltpu.SMEM((NCTX, 128), I32),
        V((NCOL, 11, BLK, 128), BF16), V((NCOL, 2, 11, BLK, 128), BF16),
        V((NCOL, 2, 11, BLK, 128), BF16), V((4, 512, EXT), BF16),
        V((4, 72, 32, 128), BF16), V((4, 72, 32, 128), BF16), V((4, UROWS, EXT), BF16),
        V((512, 256), F32), V((512, 256), F32),
        V((4, 32, BLK, UROWS), BF16), V((4, 1, UROWS), F32), V((4, 1, UROWS), F32),
        V((4, 4, 1, UROWS), F32), V((4, 4, 16, UROWS), BF16),
        V((2, SEL, BLK, UROWS), BF16), V((2, SEL, BLK, 128), BF16),
        V((NZ, 128, DI), BF16), V((DI, NZ * 128), BF16),
        V((8, 128), F32), V((NZ, 8, 128), F32), V((NZ, 128, 128), F32),
        V((SEL, BLK, DI), BF16), V((SPAN // 128, 8, 128), I32),
        V((4, 16, SPAN), F32), V((4, 16, SPAN), BF16), V((2, 16, SPAN), BF16), V((2, 16, SPAN), BF16),
        V((NZ, 128, 128), F32), V((SEL, BLK, DI), F32),
        V((SEL, 32, DI), BF16), V((SEL, 32, DI), BF16),
        V((4, 4, SEL * 2, DI), BF16), V((4, 4, SEL * 2, DI), BF16), V((2, SEL + 1, 8, DI), F32),
        V((NCTX, 32, DI), BF16), V((NCTX, 32, DI), BF16),
        V((NZ, 144, DI), BF16), V((8, 144, DI), BF16), V((8, 128), F32), V((8, 128), F32),
        V((4, 16, 512), F32), V((4, 16, 512), F32),
        dma((BLK // 2,)), dma((16,)), dma((1,)), dma((NCTX,)), dma((NCTX,)), dma((2,)),
        dma((4,)), dma((4,)), dma((8,)), dma((8,)), dma((8,)), dma((8,)),
        dma((NCOL,)), dma((NCOL,)), dma((NCOL,)), dma((NCOL,)),
        dma((2,)), dma((2,)), dma((1,)), dma((1,)), dma((4,)), dma((4,)),
        dma((16,)), dma((16,)), dma((NCTX,)), dma((NCTX,)), dma((8,)), dma((8,)), dma((1,)), dma((1,)),
    ]
    gk, gq, kl = pl.pallas_call(
        kernel,
        out_shape=[
            jax.ShapeDtypeStruct((BLK * 8, DI), F32),
            jax.ShapeDtypeStruct((8, 144, DI), BF16),
            jax.ShapeDtypeStruct((8, 128), F32),
        ],
        in_specs=[vmem, hbm, hbm, hbm, hbm, vmem],
        out_specs=[vmem] * 3,
        scratch_shapes=scratch,
        compiler_params=pltpu.CompilerParams(
            collective_id=0, has_side_effects=True, vmem_limit_bytes=62 * 1024 * 1024
        ),
        name="indexer_step",
    )(
        sel_blocks,
        latents.T.reshape(9, BLK, BLK * BLK),
        idx_keys.reshape(BLK, BLK, DI),
        mla_query.transpose(1, 2, 0).reshape(16, 9, BLK, 128),
        idx_query.reshape(128 * 8, DI),
        idx_weight.T,
    )
    grad_keys, grad_query, grad_weight, divergence = pl.pallas_call(
        unpack,
        out_shape=[
            jax.ShapeDtypeStruct((BLK, 8, DI), F32),
            jax.ShapeDtypeStruct((128, 8, DI), F32),
            jax.ShapeDtypeStruct((8, 128), F32),
            jax.ShapeDtypeStruct((16,), F32),
        ],
        in_specs=[vmem] * 3,
        out_specs=[vmem] * 4,
        name="unpack",
    )(gk, gq, kl)
    return divergence, grad_query, grad_weight.T, grad_keys


def solution(mesh):
    in_specs = (
        P("ctx", None),
        P("ctx", None),
        P("ctx", "head", None),
        P("ctx", "head", None),
        P("ctx", "head"),
        P("ctx", None),
    )
    out_specs = (
        P(("ctx", "head")),
        P("ctx", "head", None),
        P("ctx", "head"),
        P("ctx", "head", None),
    )
    return jax.shard_map(local, mesh=mesh, in_specs=in_specs, out_specs=out_specs, check_vma=False)
```

```python
import functools
import math

import jax
import jax.numpy as jnp
from jax import lax
from jax.experimental import pallas as pl
from jax.experimental.pallas import tpu as pltpu
from jax.sharding import PartitionSpec as P

MESH = pl.DeviceIdType.MESH
LAT, DI, BLK, SEL = 576, 128, 64, 32
HEADS = 128
NZ, SIDE = 8, 4
NCOL = SIDE * SIDE
NCTX = 2 * NCOL
CONTEXT, QUERIES = 131072, 4096
SPAN = SEL * BLK
EXT = 640
WIDE = EXT + DI
FLOOR = -1e30
LOW = -2e30
EXP_SCALE = 192.0**-0.5 * math.log2(math.e)
IDX_SCALE = DI**-0.5
UROWS = 512
IN_FLIGHT, LAG = 5, 6
F32, BF16, I32 = jnp.float32, jnp.bfloat16, jnp.int32

OFFSETS = [(0, 0), (0, 1), (0, 3), (1, 0), (3, 0), (1, 1), (3, 3), (1, 3), (3, 1)]
OFFSETS += [(0, 2), (2, 0), (1, 2), (2, 1), (3, 2), (2, 3), (2, 2)]
CODES = [dy * SIDE + dx for dy, dx in OFFSETS]


def pick(index, values):
    out = values[0]
    for i in range(1, len(values)):
        out = jnp.where(index == i, values[i], out)
    return out


def wrap(value, n):
    return jnp.where(value >= n, value - n, value)


def nt(a, b):
    return lax.dot_general(a, b, (((1,), (1,)), ((), ())), preferred_element_type=F32)


def kernel(
    sel_in, lat_hbm, ik_hbm, mq_hbm, iq_hbm, iw_in,
    gk_out, gq_out, kl_out,
    lat, ikv, selall, tbl, tbs, tbl1, tbs1, stage, rs, held, kbuf, qt, qbuf, qx, s_even, s_odd, prob, mrun, zrun, mchunk, wts, xbuf, xs,
    iq, iqt, iwf, iw, wcol, ikc, kpos, tq, tqb, tsib, tfar, gwacc, gkf, gsend, grecv, kz, kr, kc,
    pm, pr, gqm, gqr, klm, klr, lbuf, gbuf,
    ld_s, lq_s, li_s, sel_s, sel_r, tb_s, q_s, q_r, iq_s, iq_r, iw_s, iw_r, st_s, st_r, fw_s, fw_r,
    ts_s, ts_r, tf_s, tf_r, gs_s, gs_r, kz_s, kz_r, pm_s, pm_r, gq_s, gq_r, kl_s, kl_r,
):
    me = lax.axis_index("ctx")
    z = lax.axis_index("head")
    k, core = me // 2, me % 2
    ky, kx = k // SIDE, k % SIDE
    sib = 2 * k + 1 - core
    rho = z % 4
    half = z // 4
    src_ctx = 2 * k + rho // 2
    blk_b = rho % 2
    t_own = 2 * half + core

    def column(code, sign, c):
        dy, dx = code // SIDE, code % SIDE
        sign = sign * (1 - 2 * c)
        row = wrap(wrap(ky + sign * dy + SIDE, SIDE), SIDE)
        return row * SIDE + wrap(wrap(kx + sign * dx + SIDE, SIDE), SIDE)

    class send:
        def __init__(self, src, dst, ssem, rsem, ctx, head):
            self.own = jnp.logical_and(ctx == me, head == z)
            self.here = (src, dst, rsem)
            self.away = remote(src, dst, ssem, rsem, ctx, head)

        def start(self):
            @pl.when(self.own)
            def _():
                pltpu.make_async_copy(*self.here).start()

            @pl.when(jnp.logical_not(self.own))
            def _():
                self.away.start()

        def finish(self):
            @pl.when(jnp.logical_not(self.own))
            def _():
                self.away.wait_send()

    def send_parts(src, dst, ssem, rsem, ctx, head, early):
        own = jnp.logical_and(ctx == me, head == z)
        away = jnp.logical_not(own)
        copy = remote(src, dst, ssem, rsem, ctx, head)

        def first():
            @pl.when(own)
            def _():
                pltpu.make_async_copy(src, dst, rsem).start()

            @pl.when(jnp.logical_and(away, early))
            def _():
                copy.start()

        def second():
            @pl.when(jnp.logical_and(away, jnp.logical_not(early)))
            def _():
                copy.start()

        def done():
            @pl.when(away)
            def _():
                copy.wait_send()

        return first, second, done

    def remote(src, dst, ssem, rsem, ctx, head):
        return pltpu.make_async_remote_copy(
            src, dst, ssem, rsem, device_id={"ctx": ctx, "head": head}, device_id_type=MESH
        )

    def arrived(dst, rsem):
        pltpu.make_async_copy(dst, dst, rsem).wait()

    pending = []

    barrier = pltpu.get_barrier_semaphore()

    def greet_plane(d, carry):
        pl.semaphore_signal(
            barrier, inc=1, device_id={"ctx": wrap(me + d, NCTX), "head": z}, device_id_type=MESH
        )
        return carry

    def greet_column(d, carry):
        for c in range(2):
            pl.semaphore_signal(
                barrier, inc=1, device_id={"ctx": 2 * k + c, "head": wrap(z + d, NZ)}, device_id_type=MESH
            )
        return carry

    lax.fori_loop(1, NCTX, greet_plane, 0)
    lax.fori_loop(1, NZ, greet_column, 0)
    selall[pl.ds(me, 1), 0:2, 0:SEL] = sel_in[...].reshape(1, 2, SEL)

    def load_query(h):
        return pltpu.make_async_copy(
            mq_hbm.at[h],
            xbuf.at[h // 8, pl.ds(9 * (h // 4 % 2), 9), :, pl.ds(pl.multiple_of(h % 4 * 128, 128), 128)],
            lq_s.at[h],
        )

    def load_latents(n):
        return pltpu.make_async_copy(
            lat_hbm.at[:, :, pl.ds(pl.multiple_of(n * 128, 128), 128)], lat.at[n], ld_s.at[n]
        )

    load_ik = pltpu.make_async_copy(ik_hbm, ikv, li_s.at[0])
    for h in range(16):
        load_query(h).start()

    def start_latents(n, carry):
        load_latents(n).start()
        return carry

    lax.fori_loop(0, BLK // 2, start_latents, 0)
    load_ik.start()
    iwf[...] = iw_in[...].astype(F32)

    def turn_query(h, carry):
        tails = []
        for e in range(2):
            hh = h + 8 * e
            load_query(hh).wait()
            raw = xbuf.at[e, pl.ds(9 * (h // 4), 9), :, pl.ds(pl.multiple_of(h % 4 * 128, 128), 128)][...]
            rows = raw[0:8].reshape(512, 128).T
            for n in range(4):
                for t in range(4):
                    qt[n, pl.ds(16 * t + hh, 1)] = rows[32 * n : 32 * n + 32, 128 * t : 128 * t + 128].reshape(
                        1, 32, 128
                    )
            tails.append(raw[8])
        tail = jnp.concatenate(tails, axis=0).T
        for n in range(4):
            qt[n, pl.ds(64 + h, 1)] = tail[32 * n : 32 * n + 32, :].reshape(1, 32, 128)
        return carry

    lax.fori_loop(0, 8, turn_query, 0)
    pl.semaphore_wait(barrier, NCTX - 1 + 2 * (NZ - 1))

    def sel_copy(d):
        return remote(
            selall.at[me], selall.at[me], sel_s.at[d], sel_r.at[me], wrap(me + d, NCTX), z
        )

    def sel_start(d, carry):
        sel_copy(d).start()
        return carry

    lax.fori_loop(1, NCTX, sel_start, 0)

    far_sends = []
    for b in range(2):
        r = 2 * core + b
        d = (r - z + 8) % 4
        for hq in range(2):
            dz = pick(d, [0, 1, 2, 7] if hq == 0 else [0, 1, 6, 7])
            tcore = pick(d, [0, 0, 0, 1] if hq == 0 else [1, 0, 1, 1])
            unit = pick(d, [0, 1, 3, 1] if hq == 0 else [0, 2, 3, 2])
            first, second, done = send_parts(
                qt.at[2 * b + hq], qbuf.at[unit],
                q_s.at[2 * b + hq], q_r.at[unit], 2 * k + tcore, wrap(z + dz, NZ), d != 2,
            )
            first()
            far_sends.append(second)
            pending.append(done)
    for second in far_sends:
        second()

    def sel_wait(d, carry):
        src = wrap(me + d, NCTX)
        arrived(selall.at[src], sel_r.at[src])
        return carry

    lax.fori_loop(1, NCTX, sel_wait, 0)
    lane = lax.broadcasted_iota(I32, (NCTX, 128), 1)
    sub = lax.broadcasted_iota(I32, (NCTX, 128), 0)
    lane_f = lane.astype(F32)
    sub3 = lax.broadcasted_iota(I32, (NCTX, 8, 128), 1)

    def rows_of(b):
        return jnp.sum(jnp.where(sub3 == b, selall[...], 0).astype(F32), axis=1).astype(I32)

    def two(match, values):
        first = jnp.min(jnp.where(match, lane_f, 128.0), axis=1, keepdims=True)
        hit0 = jnp.logical_and(match, lane_f == first)
        hit1 = jnp.logical_and(match, lane_f > first)
        v0 = jnp.sum(jnp.where(hit0, values, 0.0), axis=1, keepdims=True)
        v1 = jnp.sum(jnp.where(hit1, values, 0.0), axis=1, keepdims=True)
        return v0, v1

    def lanes(columns):
        out = jnp.zeros((NCTX, 128), F32)
        for i, c in enumerate(columns):
            out = jnp.where(lane == i, c, out)
        return out

    listed = lane < SEL
    wanted = []
    for b in range(2):
        rows = rows_of(b)
        match = jnp.logical_and(listed, rows // BLK == me)
        v0, v1 = two(match, (rows % BLK + 1).astype(F32))
        wanted += [v0 - 1.0, v1 - 1.0]
    table1 = lanes(wanted)
    tbl1[...] = table1.astype(I32)
    to_smem1 = pltpu.make_async_copy(tbl1, tbs1, tb_s.at[1])
    to_smem1.start()

    to_smem1.wait()
    load_ik.wait()

    def wait_latents(n, carry):
        load_latents(n).wait()
        return carry

    lax.fori_loop(0, BLK // 2, wait_latents, 0)

    lane_b = lax.broadcasted_iota(I32, (BLK, 128), 1)

    def gather(code, into):
        ctx = 2 * column(code, 1, core) + rho // 2
        tails, odds = [], []
        for r in range(2):
            index = jnp.clip(tbs1[ctx, 2 * blk_b + r], 0, BLK - 1)
            odd = index % 2 == 1
            raw = lat[pl.ds(index // 2, 1)].reshape(9, BLK, 128)
            rows = raw[0:8].reshape(512, 128).T
            rows = jnp.where(odd, rows[BLK:, :], rows[:BLK, :])
            for t in range(4):
                into[4 * r + t] = rows[:, 128 * t : 128 * t + 128]
            tails.append(raw[8])
            odds.append(odd)
            into[9 + r] = ikv[pl.ds(index, 1)].reshape(BLK, DI)
        tail = jnp.concatenate(tails, axis=0).T.astype(F32)
        tails = [jnp.where(odd, tail[BLK:, :], tail[:BLK, :]) for odd in odds]
        into[8] = jnp.where(lane_b < BLK, tails[0], tails[1]).astype(BF16)

    def stage_copy(i):
        to = 2 * column(pick(i, CODES), 1, core) + core
        return remote(stage.at[i], rs.at[i, core], st_s.at[i], st_r.at[i], to, z)

    def stage_send(n, carry):
        i = n % NCOL
        gather(pick(i, CODES), stage.at[i])

        @pl.when(i > 0)
        def _():
            stage_copy(i).start()

        return carry

    stage_send(NCOL, 0)
    lax.fori_loop(1, IN_FLIGHT + 1, stage_send, 0)
    for b in range(2):
        for t in range(4):
            tz = 2 * core + b + 4 * (t // 2)
            tc = 2 * k + t % 2
            for copy in (
                send(
                    iq_hbm.at[pl.ds((BLK * b + 16 * t) * 8, 128)], iq.at[z],
                    iq_s.at[4 * b + t], iq_r.at[z], tc, tz,
                ),
                send(iwf, iw.at[z], iw_s.at[4 * b + t], iw_r.at[z], tc, tz),
            ):
                copy.start()
                pending.append(copy.finish)
    rs[0, pl.ds(core, 1)] = stage[0:1]

    sub8 = lax.broadcasted_iota(I32, (8, 128), 0)

    def row_of(ctx, b):
        tile = selall[pl.ds(ctx, 1)].reshape(8, 128)
        return jnp.sum(jnp.where(sub8 == b, tile, 0).astype(F32), axis=0, keepdims=True)

    def by_owner(row):
        row = jnp.broadcast_to(row.astype(I32), (NCTX, 128))
        match = jnp.logical_and(listed, row // BLK == sub)
        return two(match, row.astype(F32) + 1.0)

    def use_order(col_index, odd):
        dy = ky - col_index // SIDE
        dx = kx - col_index % SIDE
        dy, dx = jnp.where(odd, -dy, dy), jnp.where(odd, -dx, dx)
        code = ((dy + SIDE) % SIDE) * SIDE + (dx + SIDE) % SIDE
        place = jnp.zeros_like(code)
        for i, c in enumerate(CODES):
            place = jnp.where(code == c, i, place)
        return place * 2 + odd.astype(I32)

    order = use_order(sub // 2, sub % 2 == 1)
    order_lane = use_order(lane % NCTX // 2, lane % 2 == 1)
    before = jnp.where(jnp.logical_and(order_lane < order, lane < NCTX), 1.0, 0.0)[:, 0:NCTX].astype(BF16)

    def number(row):
        v0, v1 = by_owner(row)
        has0, has1 = v0 > 0.5, v1 > 0.5
        count = jnp.where(has0, 1.0, 0.0) + jnp.where(has1, 1.0, 0.0)
        count = jnp.broadcast_to(count, (NCTX, 128)).astype(BF16)
        n0 = jnp.dot(before, count, preferred_element_type=F32)
        return v0, v1, jnp.where(has0, n0, float(SEL)), jnp.where(has1, n0 + 1.0, float(SEL))

    v0, v1, n0, n1 = number(row_of(src_ctx, blk_b))
    hit0 = jnp.logical_and(lane_f == n0, listed)
    hit1 = jnp.logical_and(lane_f == n1, listed)
    slot = order.astype(F32) * 2.0

    def along(a, b):
        total = jnp.where(hit0, a, 0.0) + jnp.where(hit1, b, 0.0)
        return jnp.sum(total, axis=0, keepdims=True)

    slots = along(slot, slot + 1.0)
    blocks = along(v0 - 1.0, v1 - 1.0)
    columns = [v0, v1]
    for b in range(2):
        _, _, m0, m1 = number(row_of(me, b))
        columns += [m0, m1]
    tbl[0:NCTX, :] = lanes(columns).astype(I32)
    tbl[NCTX : NCTX + 8, :] = jnp.where(
        sub8 == 0, jnp.broadcast_to(slots, (8, 128)), jnp.broadcast_to(blocks, (8, 128))
    ).astype(I32)
    to_smem = pltpu.make_async_copy(tbl, tbs, tb_s.at[0])
    to_smem.start()
    to_smem.wait()

    def forward_copy(i):
        return remote(rs.at[i, core], rs.at[i, core], fw_s.at[i], fw_r.at[i], sib, z)

    key_off = lax.broadcasted_iota(I32, (BLK, 128), 0)
    q_base = CONTEXT - QUERIES + src_ctx * 128 + blk_b * BLK
    reach = lane_b - BLK + q_base - key_off

    def forward(i):
        @pl.when(i > 0)
        def _():
            arrived(rs.at[i, core], st_r.at[i])

        forward_copy(i).start()

    def settle(i):
        arrived(rs.at[i, 1 - core], fw_r.at[i])
        held[pl.ds(i, 1)] = rs[pl.ds(i, 1)]

    def collect(g):
        def block(j, carry):
            n = 8 * g + j
            s = jnp.clip(tbs[NCTX, n], 0, 63)
            odd = s % 2 == 1
            place = held.at[pl.ds(s // 4, 1), pl.ds(s // 2 % 2, 1)]
            at = pl.ds(pl.multiple_of(j * BLK, BLK), BLK)
            for t in range(4):
                kbuf[g, at, 128 * t : 128 * t + 128] = place[:, :, pl.ds(s % 2 * 4 + t, 1)].reshape(BLK, 128)
            tail = place[:, :, 8].reshape(BLK, 128).astype(F32)
            tail = jnp.where(odd, pltpu.roll(tail, 64, 1), tail)
            bias = jnp.where(tbs[NCTX + 1, n] * BLK > reach, FLOOR, 0.0)
            kbuf[g, at, 512:EXT] = jnp.where(lane_b < BLK, tail, bias).astype(BF16)
            ikc[pl.ds(n, 1)] = place[:, :, pl.ds(9 + s % 2, 1)].reshape(1, BLK, DI)
            return carry

        lax.fori_loop(0, 8, block, 0)

    def query_unit(u):
        arrived(qbuf.at[u], q_r.at[u])
        first_q = pick(u, [32 * core, 0, 32, 32 * core])
        row = lax.broadcasted_iota(I32, (256, 128), 0) % 32 + first_q
        col = lax.broadcasted_iota(I32, (256, 128), 1)
        hot = jnp.where(row == col - BLK, 1.0, 0.0)
        for t in range(4):
            qx[u, :, 128 * t : 128 * t + 128] = qbuf[u, 16 * t : 16 * t + 16].reshape(UROWS, 128)
        tail = qbuf[u, 64:72].reshape(256, 128).astype(F32)
        qx[u, 0:256, 512:EXT] = jnp.where(col < BLK, tail, hot).astype(BF16)
        qx[u, 256:512, 512:EXT] = jnp.where(col < BLK, pltpu.roll(tail, 64, 1), hot).astype(BF16)
        mrun[u] = jnp.full((1, UROWS), LOW, F32)
        zrun[u] = jnp.zeros((1, UROWS), F32)

    def score(u, c, h, into):
        into[...] = nt(kbuf[c], qx[u, 256 * h : 256 * h + 256, :])

    def soften(u, c, h, held_scores):
        s = held_scores[...]
        lanes_h = slice(256 * h, 256 * h + 256)
        old = mrun[u, :, lanes_h]
        new = jnp.maximum(old, jnp.max(s, axis=0, keepdims=True))
        p = jnp.exp2((s - new) * EXP_SCALE)
        zrun[u, :, lanes_h] = zrun[u, :, lanes_h] * jnp.exp2((old - new) * EXP_SCALE) + jnp.sum(
            p, axis=0, keepdims=True
        )
        mrun[u, :, lanes_h] = new
        mchunk[c, u, :, lanes_h] = new
        prob[c, pl.ds(8 * u, 8), :, lanes_h] = p.astype(BF16).reshape(8, BLK, 256)

    def group(g):
        collect(g)

        def step(u, carry):
            score(u, g, 1, s_odd)
            soften(u, g, 0, s_even)
            score(jnp.minimum(u + 1, 3), g, 0, s_even)
            soften(u, g, 1, s_odd)
            return carry

        score(0, g, 0, s_even)
        lax.fori_loop(0, 4, step, 0)

    def flow(i, carry):
        @pl.when(i < NCOL)
        def _():
            stage_copy(i - IN_FLIGHT).wait_send()
            stage_send(i, 0)

        @pl.when(i >= LAG)
        def _():
            forward(i - LAG)

        @pl.when(i > LAG)
        def _():
            settle(i - LAG - 1)

        return carry

    def unit(u, carry):
        query_unit(u)
        return carry

    lax.fori_loop(IN_FLIGHT + 1, 14, flow, 0)
    lax.fori_loop(0, 4, unit, 0)
    def positions(i, carry):
        l8 = lax.broadcasted_iota(I32, (8, 128), 1)
        a, b = tbs[NCTX + 1, 2 * i] * BLK, tbs[NCTX + 1, 2 * i + 1] * BLK
        kpos[pl.ds(i, 1)] = (jnp.where(l8 < BLK, a, b) + l8 % BLK).reshape(1, 8, 128)
        return carry

    lax.fori_loop(0, SPAN // 128, positions, 0)
    own_q = lax.broadcasted_iota(I32, (128, 128), 0) // 8 + BLK * blk_b + 16 * t_own
    own_q = own_q == lax.broadcasted_iota(I32, (128, 128), 1)

    def prepare(s, carry):
        arrived(iq.at[s], iq_r.at[s])
        arrived(iw.at[s], iw_r.at[s])
        w = jnp.broadcast_to(iw[s].reshape(1, 8, 128), (16, 8, 128)).reshape(128, 128)
        w = jnp.sum(jnp.where(own_q, w, 0.0), axis=1, keepdims=True)
        wcol[s] = jnp.broadcast_to(w * IDX_SCALE, (128, 128))
        iqt[:, pl.ds(pl.multiple_of(128 * s, 128), 128)] = iq[s].astype(F32).T.astype(BF16)
        return carry

    lax.fori_loop(0, NZ, prepare, 0)

    lax.fori_loop(14, 10 + LAG, flow, 0)
    settle(9)

    def arrive_and_score(g, carry):
        @pl.when(g > 0)
        def _():
            settle(8 + 2 * g)
            settle(9 + 2 * g)

        @pl.when(g < 3)
        def _():
            forward(10 + 2 * g)
            forward(11 + 2 * g)

        group(g)
        return carry

    lax.fori_loop(0, 4, arrive_and_score, 0)

    for u in range(4):
        scale = 1.0 / (zrun[u] * HEADS)
        for c in range(4):
            w = jnp.exp2((mchunk[c, u] - mrun[u]) * EXP_SCALE) * scale
            wts[c, u] = jnp.broadcast_to(w, (16, UROWS)).astype(BF16)

    def compact(i, carry):
        c, j = i // 8, i % 8

        def part(u):
            p = prob[pl.ds(c, 1), pl.ds(8 * u + j, 1)].reshape(4, 16, UROWS)
            return p * wts[pl.ds(c, 1), pl.ds(u, 1)].reshape(1, 16, UROWS)

        def narrow(p):
            p = p.reshape(BLK, UROWS).astype(F32)
            p = (p[:, 0:128] + p[:, 128:256]) + (p[:, 256:384] + p[:, 384:512])
            return p.astype(BF16).reshape(1, BLK, 128)

        xs[0, pl.ds(i, 1)] = narrow(part(0) + part(3) + part(1 + core))
        xs[1, pl.ds(i, 1)] = narrow(part(2 - core))
        return carry

    lax.fori_loop(0, SEL, compact, 0)
    fold = jnp.where(
        lax.broadcasted_iota(I32, (32, 128), 0) == lax.broadcasted_iota(I32, (32, 128), 1) % 32, 1.0, 0.0
    ).astype(BF16)
    for x in range(2):
        part = nt(fold, xs[x].reshape(SPAN, 128))
        h = core if x == 0 else 1 - core
        tq[pl.ds(2 * h, 2)] = part.reshape(2, 16, SPAN)
        tqb[pl.ds(2 * h, 2)] = part.astype(BF16).reshape(2, 16, SPAN)
    sib_copies = [
        remote(tqb.at[1 - core + 2 * h], tsib.at[h], ts_s.at[h], ts_r.at[h], sib, z) for h in range(2)
    ]
    for copy in sib_copies:
        copy.start()

    TILE = 512

    def dots_of(s, kt):
        keys = ikc[pl.ds(kt * (TILE // BLK), TILE // BLK)].reshape(TILE, DI)
        return nt(iq[s], keys)

    def logit_tile(kt, carry):
        acc = jnp.zeros((128, TILE), F32)
        for s in range(NZ):
            w = jnp.concatenate([wcol[s]] * (TILE // 128), axis=1)
            acc = acc + w * jnp.maximum(dots_of(s, kt), 0.0)
        lbuf[kt] = jnp.sum(acc.reshape(16, 8, TILE), axis=1)
        return carry

    lax.fori_loop(0, SPAN // TILE, logit_tile, 0)

    q_pos = q_base + 16 * t_own + lax.broadcasted_iota(I32, (16, 128), 0)
    visible = jnp.concatenate(
        [jnp.concatenate([kpos[i]] * 2, axis=0) <= q_pos for i in range(SPAN // 128)], axis=1
    )

    for h, copy in enumerate(sib_copies):
        arrived(tsib.at[h], ts_r.at[h])
        copy.wait_send()
    far = 1 - half
    mine = tq[pl.ds(2 * half + core, 1)].reshape(16, SPAN) + tsib[pl.ds(half, 1)].reshape(16, SPAN).astype(F32)
    other = tq[pl.ds(2 * far + core, 1)].reshape(16, SPAN) + tsib[pl.ds(far, 1)].reshape(16, SPAN).astype(F32)
    tfar[0] = other.astype(BF16)
    far_copy = remote(tfar.at[0], tfar.at[1], tf_s.at[0], tf_r.at[0], me, wrap(z + 4, NZ))
    far_copy.start()

    for finish in pending:
        finish()

    def drain_sel(d, carry):
        sel_copy(d).wait_send()
        return carry

    def drain_stage(i, carry):
        stage_copy(i).wait_send()
        return carry

    def drain_forward(i, carry):
        forward_copy(i).wait_send()
        return carry

    lax.fori_loop(1, NCTX, drain_sel, 0)
    lax.fori_loop(NCOL - IN_FLIGHT, NCOL, drain_stage, 0)
    lax.fori_loop(0, NCOL, drain_forward, 0)
    logits = jnp.concatenate([lbuf[kt] for kt in range(SPAN // TILE)], axis=1)
    masked = jnp.where(visible, logits, FLOOR)
    shifted = masked - jnp.max(masked, axis=1, keepdims=True)
    log_norm = jnp.log(jnp.sum(jnp.exp(shifted), axis=1, keepdims=True))
    log_ratio = shifted - log_norm
    predicted = jnp.where(visible, jnp.exp(log_ratio), 0.0)
    arrived(tfar.at[1], tf_r.at[0])
    target = mine + tfar[1].astype(F32)
    positive = target > 0.0
    entropy = jnp.sum(
        jnp.where(positive, target * jnp.log(jnp.where(positive, target, 1.0)), 0.0), axis=1, keepdims=True
    )
    cross = jnp.sum(jnp.where(visible, target * log_ratio, 0.0), axis=1, keepdims=True)
    gradient = jnp.where(visible, SPAN * (predicted - target), 0.0).astype(BF16).astype(F32)
    divergence = entropy - cross
    spot = lax.broadcasted_iota(I32, (16, 128), 0) == lax.broadcasted_iota(I32, (16, 128), 1)
    klm[...] = jnp.broadcast_to(
        jnp.sum(jnp.where(spot, divergence, 0.0), axis=0, keepdims=True), (8, 128)
    )
    kl_send = send(klm, klr, kl_s.at[0], kl_r.at[0], src_ctx, 4 * blk_b + t_own)
    kl_send.start()

    KB = TILE // BLK

    def swap(kt):
        part = pl.ds(kt * KB, KB)
        return remote(gsend.at[part], grecv.at[part], gs_s.at[kt], gs_r.at[kt], sib, z)

    def kz_send(kt, t):
        to = 2 * blk_b + half
        return send(
            kz.at[t, kt], kr.at[to, kt], kz_s.at[4 * t + kt], kz_r.at[4 * to + kt], src_ctx, 4 * core + t
        )

    def cores_sum(kt):
        here = pl.ds(kt * KB, KB)
        arrived(grecv.at[here], gs_r.at[kt])
        both = gkf[here, pl.ds(32 * core, 32), :] + grecv[here].astype(F32)
        for t in range(4):
            kz[t, pl.ds(kt, 1)] = both[:, 8 * t : 8 * t + 8, :].reshape(1, KB * 8, DI).astype(BF16)
            kz_send(kt, t).start()

    for kt in range(SPAN // TILE):
        gbuf[kt] = gradient[:, kt * TILE : (kt + 1) * TILE]

    def backward(kt, carry):
        g = gbuf[kt]
        g = jnp.broadcast_to(g.reshape(16, 1, TILE), (16, 8, TILE)).reshape(128, TILE)
        for s in range(NZ):
            dots = dots_of(s, kt)
            weighted = g * jnp.maximum(dots, 0.0)
            lanesum = weighted[:, 0:128]
            for i in range(1, TILE // 128):
                lanesum = lanesum + weighted[:, 128 * i : 128 * (i + 1)]
            gwacc[s] = jnp.where(kt == 0, 0.0, gwacc[s]) + lanesum
            w = jnp.concatenate([wcol[s]] * (TILE // 128), axis=1)
            prob[kt, 2 * s : 2 * s + 2] = (
                jnp.where(dots > 0.0, g * w, 0.0).astype(BF16).reshape(2, BLK, TILE)
            )
        part = jnp.dot(iqt[...], prob[kt, 0 : 2 * NZ].reshape(NZ * 128, TILE), preferred_element_type=F32)
        here = pl.ds(kt * KB, KB)
        gkf[here] = part.T.reshape(KB, BLK, DI)
        gsend[here] = gkf[here, pl.ds(32 * (1 - core), 32), :].astype(BF16)
        swap(kt).start()

        @pl.when(kt > 0)
        def _():
            cores_sum(kt - 1)

        return carry

    lax.fori_loop(0, SPAN // TILE, backward, 0)

    unspread = jnp.where(
        lax.broadcasted_iota(I32, (16, 128), 0) == lax.broadcasted_iota(I32, (16, 128), 1) // 8, 1.0, 0.0
    )
    diag_j = lax.broadcasted_iota(I32, (128, 128), 0) % 8 == lax.broadcasted_iota(I32, (128, 128), 1)
    def query_grad(s, carry):
        factor = jnp.concatenate(
            [prob[kt, pl.ds(2 * s, 2)].reshape(128, TILE) for kt in range(SPAN // TILE)], axis=1
        )
        gq = jnp.dot(factor, ikc[...].reshape(SPAN, DI), preferred_element_type=F32)
        gw = jnp.sum(gwacc[s], axis=1, keepdims=True) * IDX_SCALE
        gw = jnp.dot(
            unspread, jnp.where(diag_j, gw, 0.0), preferred_element_type=F32, precision=lax.Precision.HIGHEST
        )
        gqm[pl.ds(s, 1), 0:128, :] = gq.astype(BF16).reshape(1, 128, DI)
        gqm[pl.ds(s, 1), 128:144, :] = gw.astype(BF16).reshape(1, 16, DI)
        return carry

    lax.fori_loop(0, NZ, query_grad, 0)
    cores_sum(SPAN // TILE - 1)

    def gq_send(s):
        return send(gqm.at[s], gqr.at[4 * blk_b + t_own], gq_s.at[s], gq_r.at[4 * blk_b + t_own], src_ctx, s)

    def gq_start(s, carry):
        gq_send(s).start()
        return carry

    lax.fori_loop(0, NZ, gq_start, 0)
    for kt in range(SPAN // TILE):
        swap(kt).wait_send()
    for b in range(2):
        for h in range(2):
            for kt in range(SPAN // TILE):
                arrived(kr.at[2 * b + h, kt], kz_r.at[4 * (2 * b + h) + kt])
        total = kr[2 * b].astype(F32) + kr[2 * b + 1].astype(F32)
        kc[b, 0:SEL] = total.reshape(SEL, 8, DI)
        kc[b, SEL : SEL + 1] = jnp.zeros((1, 8, DI), F32)

    def owner_copy(o):
        return remote(pm.at[o], pr.at[me], pm_s.at[o], pm_r.at[me], o, z)

    def owner_block(o):
        parts = []
        for b in range(2):
            for r in range(2):
                index = jnp.clip(tbs[o, 2 + 2 * b + r], 0, SEL)
                parts.append(kc[pl.ds(b, 1), pl.ds(index, 1)].reshape(8, DI))
        return jnp.concatenate(parts, axis=0).astype(BF16)

    def owner_of(i):
        return wrap(me + i, NCTX)

    def owner_send(i, carry):
        o = owner_of(i)
        pm[pl.ds(o, 1)] = owner_block(o).reshape(1, 32, DI)
        owner_copy(o).start()
        return carry

    lax.fori_loop(1, NCTX, owner_send, 0)
    pr[pl.ds(me, 1)] = owner_block(me).reshape(1, 32, DI)

    col = lax.broadcasted_iota(I32, (128, 1024), 1)
    expand = jnp.where(col % 32 // 8 == lax.broadcasted_iota(I32, (128, 1024), 0), 1.0, 0.0).astype(BF16)
    wide = jnp.dot(table1.astype(BF16), expand, preferred_element_type=F32)
    col = lax.broadcasted_iota(I32, (NCTX, 1024), 1)
    wide = jnp.where(col // 32 == lax.broadcasted_iota(I32, (NCTX, 1024), 0), wide * 8.0, 0.0)
    code = jnp.sum(wide, axis=0, keepdims=True) + (
        lax.broadcasted_iota(I32, (1, 1024), 1) % 8
    ).astype(F32)
    row = lax.broadcasted_iota(I32, (128, 1024), 0).astype(F32)

    def sum_blocks(i, carry):
        hot = jnp.where(row == code - (128 * i).astype(F32), 1.0, 0.0).astype(BF16)
        gk_out[pl.ds(pl.multiple_of(128 * i, 128), 128), :] = jnp.dot(
            hot, pr[...].reshape(1024, DI), preferred_element_type=F32
        )
        return carry


    arrived(klr, kl_r.at[0])
    kl_out[...] = klr[...]
    for i in range(8):
        arrived(gqr.at[i], gq_r.at[i])
        gq_out[i] = gqr[i]

    def owner_wait(i, carry):
        o = owner_of(i)
        arrived(pr.at[o], pm_r.at[o])
        owner_copy(o).wait_send()
        return carry

    lax.fori_loop(1, NCTX, owner_wait, 0)
    lax.fori_loop(0, 4, sum_blocks, 0)

    kl_send.finish()
    far_copy.wait_send()

    def drain_gradients(s, carry):
        gq_send(s).finish()
        for t in range(2):
            kz_send(s % 4, s // 4 * 2 + t).finish()
        return carry

    lax.fori_loop(0, NZ, drain_gradients, 0)


def unpack(gk, gq, kl, gk_out, gq_out, gw_out, kl_out):
    gk_out[...] = gk[...].reshape(BLK, 8, DI)
    weights = []
    for i in range(8):
        gq_out[16 * i : 16 * (i + 1)] = gq[i, 0:128, :].astype(F32).reshape(16, 8, DI)
        weights.append(gq[i, 128:144, :].astype(F32))
    gw_out[...] = jnp.concatenate(weights, axis=0).T[0:8, :]
    kl_out[...] = kl[0, 0:16]


def local(latents, idx_keys, mla_query, idx_query, idx_weight, sel_blocks):
    V = pltpu.VMEM
    dma = pltpu.SemaphoreType.DMA
    hbm = pl.BlockSpec(memory_space=pl.ANY)
    vmem = pl.BlockSpec(memory_space=pltpu.VMEM)
    scratch = [
        V((BLK // 2, 9, BLK, 128), BF16), V((BLK, BLK, DI), BF16), V((NCTX, 8, 128), I32),
        V((NCTX + 8, 128), I32), pltpu.SMEM((NCTX + 8, 128), I32),
        V((NCTX, 128), I32), pltpu.SMEM((NCTX, 128), I32),
        V((NCOL, 11, BLK, 128), BF16), V((NCOL, 2, 11, BLK, 128), BF16),
        V((NCOL, 2, 11, BLK, 128), BF16), V((4, 512, EXT), BF16),
        V((4, 72, 32, 128), BF16), V((4, 72, 32, 128), BF16), V((4, UROWS, EXT), BF16),
        V((512, 256), F32), V((512, 256), F32),
        V((4, 32, BLK, UROWS), BF16), V((4, 1, UROWS), F32), V((4, 1, UROWS), F32),
        V((4, 4, 1, UROWS), F32), V((4, 4, 16, UROWS), BF16),
        V((2, SEL, BLK, UROWS), BF16), V((2, SEL, BLK, 128), BF16),
        V((NZ, 128, DI), BF16), V((DI, NZ * 128), BF16),
        V((8, 128), F32), V((NZ, 8, 128), F32), V((NZ, 128, 128), F32),
        V((SEL, BLK, DI), BF16), V((SPAN // 128, 8, 128), I32),
        V((4, 16, SPAN), F32), V((4, 16, SPAN), BF16), V((2, 16, SPAN), BF16), V((2, 16, SPAN), BF16),
        V((NZ, 128, 128), F32), V((SEL, BLK, DI), F32),
        V((SEL, 32, DI), BF16), V((SEL, 32, DI), BF16),
        V((4, 4, SEL * 2, DI), BF16), V((4, 4, SEL * 2, DI), BF16), V((2, SEL + 1, 8, DI), F32),
        V((NCTX, 32, DI), BF16), V((NCTX, 32, DI), BF16),
        V((NZ, 144, DI), BF16), V((8, 144, DI), BF16), V((8, 128), F32), V((8, 128), F32),
        V((4, 16, 512), F32), V((4, 16, 512), F32),
        dma((BLK // 2,)), dma((16,)), dma((1,)), dma((NCTX,)), dma((NCTX,)), dma((2,)),
        dma((4,)), dma((4,)), dma((8,)), dma((8,)), dma((8,)), dma((8,)),
        dma((NCOL,)), dma((NCOL,)), dma((NCOL,)), dma((NCOL,)),
        dma((2,)), dma((2,)), dma((1,)), dma((1,)), dma((4,)), dma((4,)),
        dma((16,)), dma((16,)), dma((NCTX,)), dma((NCTX,)), dma((8,)), dma((8,)), dma((1,)), dma((1,)),
    ]
    gk, gq, kl = pl.pallas_call(
        kernel,
        out_shape=[
            jax.ShapeDtypeStruct((BLK * 8, DI), F32),
            jax.ShapeDtypeStruct((8, 144, DI), BF16),
            jax.ShapeDtypeStruct((8, 128), F32),
        ],
        in_specs=[vmem, hbm, hbm, hbm, hbm, vmem],
        out_specs=[vmem] * 3,
        scratch_shapes=scratch,
        compiler_params=pltpu.CompilerParams(
            collective_id=0, has_side_effects=True, vmem_limit_bytes=62 * 1024 * 1024
        ),
        name="indexer_step",
    )(
        sel_blocks,
        latents.T.reshape(9, BLK, BLK * BLK),
        idx_keys.reshape(BLK, BLK, DI),
        mla_query.transpose(1, 2, 0).reshape(16, 9, BLK, 128),
        idx_query.reshape(128 * 8, DI),
        idx_weight.T,
    )
    grad_keys, grad_query, grad_weight, divergence = pl.pallas_call(
        unpack,
        out_shape=[
            jax.ShapeDtypeStruct((BLK, 8, DI), F32),
            jax.ShapeDtypeStruct((128, 8, DI), F32),
            jax.ShapeDtypeStruct((8, 128), F32),
            jax.ShapeDtypeStruct((16,), F32),
        ],
        in_specs=[vmem] * 3,
        out_specs=[vmem] * 4,
        name="unpack",
    )(gk, gq, kl)
    return divergence, grad_query, grad_weight.T, grad_keys


def solution(mesh):
    in_specs = (
        P("ctx", None),
        P("ctx", None),
        P("ctx", "head", None),
        P("ctx", "head", None),
        P("ctx", "head"),
        P("ctx", None),
    )
    out_specs = (
        P(("ctx", "head")),
        P("ctx", "head", None),
        P("ctx", "head"),
        P("ctx", "head", None),
    )
    return jax.shard_map(local, mesh=mesh, in_specs=in_specs, out_specs=out_specs, check_vma=False)
```
